32 devices in a mesh: comp: 2 (over x), mr: 16 (over z, y, core).
Axes of the slice: x: 2, y: 2, z: 4, core: 2. Of those that a mesh axis runs over, the one named last changes fastest.
Arguments:
- spectrum: float32 [2, 1024, 2, 64, 512], P('comp', 'mr'), may hold values from -6 to 6
- radial_basis: bfloat16 [1024, 1024, 512], P('mr'), may hold values from -0.25 to 0.25
- cutoff: int32 [1024], P('mr'), may hold values from 128 to 512, as said below
- couplings: float32 [2, 2], replicated, may hold values from 0.5 to 1.5
- trap_potential: float32 [1024], replicated, may hold values from 0 to 2
- weights: float32 [1024], replicated, may hold values from 0.25 to 0.75
Outputs:
- evolved: float32 [2, 1024, 2, 64, 512], P('comp', 'mr')
The draws below stay inside these ranges and needn't reach their ends.
Inputs may be any that keep to these rules, and one draw needn't show every extreme that they name: cutoff[m] is the number of Laguerre degrees kept for angular mode m; degrees from cutoff[m] on are dropped.
All inputs are finite; a program needn't handle non-finite values.
Results may differ from the reference program's by a relative error of at most 0.0089.
Values may be sent and summed in bfloat16 or wider, within the bound.
No kernel may reach another device: no remote copies, remote signals or barrier semaphores. Data moves between devices by JAX's collectives and lax.ppermute only.
A program may use at most 320 MiB of HBM per device.

```python
import math
import jax
import jax.numpy as jnp
from jax import lax

M = 1024
R = 1024
NL = 512
Z = 64


def draw_cutoff(key, part):
    positions = jnp.arange(M, dtype=jnp.int32)
    signed = jnp.where(positions < M // 2, positions, positions - M)
    magnitude = jnp.abs(signed).astype(jnp.int32)
    sloped = NL - magnitude * (NL // 2) // (M // 2)
    jitter = jax.random.randint(key, (M,), 0, max(NL // 8, 1), dtype=jnp.int32)
    values = sloped - jitter
    values = jnp.where(magnitude == 0, NL, values)
    values = jnp.where(magnitude == M // 2, NL // 4, values)
    return values.astype(jnp.int32)


def block_scale(key, dims, split, least, high):
    def one(axis_at, blocks):
        draws = jax.random.uniform(jax.random.fold_in(jax.random.fold_in(key, 6), axis_at), (blocks,), jnp.float32, least / len(split), high / len(split))
        return jnp.repeat(jnp.exp(draws), dims[axis_at] // blocks).reshape((-1,) + (1,) * (len(dims) - axis_at - 1))

    level = one(*split[0])
    for cut in split[1:]:
        level = level * one(*cut)
    return level


def normal_values(key, shape, spread, limit, cuts=(), kind=jnp.bfloat16):
    gain = block_scale(key, shape, cuts, -0.22, 0.18) if cuts else 1.0
    entries = jax.random.normal(key, shape, jnp.float32) * spread * gain
    return jnp.minimum(jnp.maximum(entries, -limit), limit).astype(kind)


def setup_inputs(seed: int = 0) -> dict:
    arg_keys = jax.random.split(jax.random.key(seed), 7)
    return {
        "spectrum": normal_values(arg_keys[0], (2, M, 2, Z, NL), 1.0, 6.0, ((0, 2), (1, 16)), jnp.float32),
        "radial_basis": normal_values(arg_keys[1], (M, R, NL), NL ** -0.5, 0.25, ((0, 16),)),
        "cutoff": draw_cutoff(jax.random.fold_in(arg_keys[6], 71), 0),
        "couplings": jnp.clip(jax.random.uniform(arg_keys[3], (2, 2), jnp.float32, 0.5, 1.5), 0.5, 1.5),
        "trap_potential": jnp.clip(jax.random.uniform(arg_keys[4], (R,), jnp.float32, 0.0, 2.0), 0.0, 2.0),
        "weights": jnp.clip(jax.random.uniform(arg_keys[5], (R,), jnp.float32, 0.25, 0.75), 0.25, 0.75),
    }


TIMESTEP = 0.5
ROTATION = 0.7

def spectral_tables(mode_total):
    ordinal = jnp.arange(mode_total, dtype=jnp.int32)
    product = ordinal[:, None] * ordinal[None, :] % mode_total
    angles = product.astype(jnp.float32) * (2.0 * math.pi / mode_total)
    normalizer = 1.0 / math.sqrt(mode_total)
    return ((jnp.cos(angles) * normalizer).astype(jnp.bfloat16), (jnp.sin(angles) * normalizer).astype(jnp.bfloat16))

def rotate(real_part, imag_part, phase_angle):
    cosine = jnp.cos(phase_angle)
    sine_value = jnp.sin(phase_angle)
    return (real_part * cosine + imag_part * sine_value, imag_part * cosine - real_part * sine_value)

def reference(spectrum, radial_basis, cutoff, couplings, trap_potential, weights):
    mode_ids = jnp.arange(M, dtype=jnp.int32)
    signed = jnp.where(mode_ids < M // 2, mode_ids, mode_ids - M).astype(jnp.float32)
    degree_ids = jnp.arange(NL, dtype=jnp.int32)
    energy = 2.0 * degree_ids.astype(jnp.float32)[None, :] + (jnp.abs(signed) + 1.0 - ROTATION * signed)[:, None]
    kinetic_phase = TIMESTEP * energy
    kept_mask = (degree_ids[None, :] < cutoff[:, None]).astype(jnp.float32)
    spin_real, spin_imag = rotate(spectrum[:, :, 0], spectrum[:, :, 1], kinetic_phase[None, :, None, :])
    coeffs = (jnp.stack([spin_real, spin_imag], 2) * kept_mask[None, :, None, None, :]).astype(jnp.bfloat16)
    per_mode = coeffs.transpose(1, 0, 2, 3, 4).reshape(M, 4 * Z, NL)

    def synthesize(operands):
        return jnp.dot(operands[0], operands[1].T, preferred_element_type=jnp.float32).astype(jnp.bfloat16)
    radial = lax.map(synthesize, (per_mode, radial_basis))
    block_count = 8
    block_rows = R // block_count
    blocks = radial.reshape(M, 4 * Z, block_count, block_rows).transpose(2, 0, 1, 3)
    cosine_table, sine_table = spectral_tables(M)

    def physical(operands):
        block_field, trap_rows, weight_rows = operands
        flattened = block_field.reshape(M, 4 * Z * block_rows)
        cosine_term = jnp.dot(cosine_table, flattened, preferred_element_type=jnp.float32).reshape(M, 2, 2, Z, block_rows)
        sine_term = jnp.dot(sine_table, flattened, preferred_element_type=jnp.float32).reshape(M, 2, 2, Z, block_rows)
        real_part = cosine_term[:, :, 0] - sine_term[:, :, 1]
        imag_part = sine_term[:, :, 0] + cosine_term[:, :, 1]
        density = real_part * real_part + imag_part * imag_part
        partner = density[:, ::-1]
        phase_angle = TIMESTEP * (couplings[:, 0][None, :, None, None] * density + couplings[:, 1][None, :, None, None] * partner + trap_rows[None, None, None, :])
        kick_real, kick_imag = rotate(real_part, imag_part, phase_angle)
        kicked = jnp.stack([kick_real, kick_imag], 2).astype(jnp.bfloat16).reshape(M, 4 * Z * block_rows)
        cosine_back = jnp.dot(cosine_table.T, kicked, preferred_element_type=jnp.float32).reshape(M, 2, 2, Z, block_rows)
        sine_back = jnp.dot(sine_table.T, kicked, preferred_element_type=jnp.float32).reshape(M, 2, 2, Z, block_rows)
        back_real = cosine_back[:, :, 0] + sine_back[:, :, 1]
        back_imag = cosine_back[:, :, 1] - sine_back[:, :, 0]
        weighted = jnp.stack([back_real, back_imag], 2) * weight_rows
        return weighted.astype(jnp.bfloat16).reshape(M, 4 * Z, block_rows)
    returned = lax.map(physical, (blocks, trap_potential.reshape(block_count, block_rows), weights.reshape(block_count, block_rows)))
    returned = returned.transpose(1, 2, 0, 3).reshape(M, 4 * Z, R)

    def analyze(operands):
        return jnp.dot(operands[0], operands[1], preferred_element_type=jnp.float32)
    evolved = lax.map(analyze, (returned, radial_basis)).reshape(M, 2, 2, Z, NL) * kept_mask[:, None, None, None, :]
    return evolved.transpose(1, 0, 2, 3, 4)
```

```python
import functools
import math

import jax
import jax.numpy as jnp
import numpy as np
from jax import lax
from jax.experimental import pallas as pl
from jax.experimental.pallas import tpu as pltpu
from jax.sharding import PartitionSpec as P

TIMESTEP = 0.5
ROTATION = 0.7
VMEM_LIMIT = 56 * 1024 * 1024
CHUNK_EIGHTHS = (2, 2, 2, 2)
MODE_BLOCK = 16


def spectral_tables(mode_total):
    ordinal = jnp.arange(mode_total, dtype=jnp.int32)
    product = ordinal[:, None] * ordinal[None, :] % mode_total
    angles = product.astype(jnp.float32) * (2.0 * math.pi / mode_total)
    normalizer = 1.0 / math.sqrt(mode_total)
    cosine = (jnp.cos(angles) * normalizer).astype(jnp.bfloat16)
    sine = (jnp.sin(angles) * normalizer).astype(jnp.bfloat16)
    return jnp.concatenate([cosine, sine], axis=1)


def half_turn_series():
    grid = np.cos(np.linspace(0.0, np.pi, 4001)) * 0.25
    grid = np.sort(np.concatenate([grid + 0.25, -(grid + 0.25)]))
    grid = grid[np.abs(grid) > 1e-9]
    square = grid * grid
    cheb = np.polynomial.chebyshev.Chebyshev
    sine = cheb.fit(square, np.sin(np.pi * grid) / grid, 4, domain=[0.0, 0.25])
    cosine = cheb.fit(square, np.cos(np.pi * grid), 5, domain=[0.0, 0.25])
    poly = np.polynomial.polynomial.Polynomial
    return (
        [float(v) for v in sine.convert(kind=poly).coef],
        [float(v) for v in cosine.convert(kind=poly).coef],
    )


SINE_SERIES, COSINE_SERIES = half_turn_series()


def horner(series, square):
    total = jnp.full_like(square, series[-1])
    for term in reversed(series[:-1]):
        total = total * square + term
    return total


def cos_sin_of_turns(turns):
    rest = turns - jnp.round(turns)
    square = rest * rest
    sine = rest * horner(SINE_SERIES, square)
    cosine = horner(COSINE_SERIES, square)
    twice = sine + sine
    return 1.0 - twice * sine, twice * cosine


def swap_halves(value):
    return pltpu.roll(value, value.shape[-1] // 2, value.ndim - 1)


def first_synthesis_kernel(
    block, planes, spectrum_ref, cos_ref, sin_ref, basis_ref, coeffs_ref, out_ref, stage
):
    radii = basis_ref.shape[1]
    for i in range(block):
        cosine = cos_ref[i : i + 1, :]
        sine = sin_ref[i : i + 1, :]
        real = spectrum_ref[i, 0]
        imag = spectrum_ref[i, 1]
        coeffs = jnp.concatenate(
            [real * cosine + imag * sine, imag * cosine - real * sine], axis=0
        ).astype(jnp.bfloat16)
        coeffs_ref[i] = coeffs
        stage[pl.ds(i, radii, stride=block), :] = lax.dot_general(
            basis_ref[i], coeffs, (((1,), (1,)), ((), ())), preferred_element_type=jnp.float32
        )
    out_ref[...] = stage[...].reshape(radii, block, 2 * planes).astype(jnp.bfloat16)


def synthesis_kernel(block, coeffs_ref, basis_ref, out_ref, stage):
    radii = basis_ref.shape[1]
    for i in range(block):
        stage[pl.ds(i, radii, stride=block), :] = lax.dot_general(
            basis_ref[i],
            coeffs_ref[i],
            (((1,), (1,)), ((), ())),
            preferred_element_type=jnp.float32,
        )
    out_ref[...] = stage[...].reshape(out_ref.shape).astype(jnp.bfloat16)


def physical_kernel(tile, trap_ref, weight_ref, lanes_ref, table_ref, x_ref, out_ref, work, kick):
    row = pl.program_id(0)
    width, local_modes, lanes = x_ref.shape[1], x_ref.shape[3], x_ref.shape[4]
    total = width * local_modes
    half = lanes // 2
    group = tile // local_modes
    first = lax.broadcasted_iota(jnp.int32, (tile, lanes), 1) < half
    for t in range(total // tile):
        rows = pl.ds(t * tile, tile)
        low = x_ref[0, t * group : (t + 1) * group, 0].reshape(tile, lanes).astype(jnp.float32)
        high = x_ref[1, t * group : (t + 1) * group, 0].reshape(tile, lanes).astype(jnp.float32)
        real = jnp.where(first, low, swap_halves(high)).astype(jnp.bfloat16)
        imag = jnp.where(first, swap_halves(low), high)
        work[rows, :lanes] = real
        work[rows, lanes:] = imag.astype(jnp.bfloat16)
        lower_rows = pl.ds(total + t * tile, tile)
        work[lower_rows, :lanes] = (-imag).astype(jnp.bfloat16)
        work[lower_rows, lanes:] = real
    strength = lanes_ref[0:1, :]
    cross = lanes_ref[1:2, :]
    trap = trap_ref[row]
    weight = weight_ref[row]

    for t in range(total // tile):
        rows = pl.ds(t * tile, tile)
        psi = jnp.dot(table_ref[rows, :], work[...], preferred_element_type=jnp.float32)
        real, imag = psi[:, :lanes], psi[:, lanes:]
        density = real * real + imag * imag
        turns = strength * density + cross * swap_halves(density) + trap
        cosine, sine = cos_sin_of_turns(turns)
        kick_real = (real * cosine + imag * sine).astype(jnp.bfloat16)
        kick_imag = imag * cosine - real * sine
        kick[rows, :lanes] = kick_real
        kick[rows, lanes:] = kick_imag.astype(jnp.bfloat16)
        lower_rows = pl.ds(total + t * tile, tile)
        kick[lower_rows, :lanes] = kick_imag.astype(jnp.bfloat16)
        kick[lower_rows, lanes:] = (-(real * cosine + imag * sine)).astype(jnp.bfloat16)

    for t in range(total // tile):
        rows = pl.ds(t * tile, tile)
        back = jnp.dot(table_ref[rows, :], kick[...], preferred_element_type=jnp.float32) * weight
        real, imag = back[:, :lanes], back[:, lanes:]
        low = jnp.where(first, real, swap_halves(imag)).astype(jnp.bfloat16)
        high = jnp.where(first, swap_halves(real), imag).astype(jnp.bfloat16)
        out_ref[0, t * group : (t + 1) * group, 0] = low.reshape(group, local_modes, lanes)
        out_ref[1, t * group : (t + 1) * group, 0] = high.reshape(group, local_modes, lanes)


def analysis_kernel(block, first, last, *refs):
    if first:
        fields_ref, basis_ref, kept_ref, out_ref, stage = refs
        held_ref = None
    else:
        fields_ref, basis_ref, kept_ref, held_ref, out_ref, stage = refs
    radii = basis_ref.shape[1]
    stage[...] = fields_ref[...].astype(jnp.float32).reshape(stage.shape)
    for i in range(block):
        field = stage[pl.ds(i, radii, stride=block), :].astype(jnp.bfloat16)
        part = lax.dot_general(
            field, basis_ref[i], (((0,), (0,)), ((), ())), preferred_element_type=jnp.float32
        )
        if not first:
            part = part + held_ref[i]
        if last:
            part = part * kept_ref[i : i + 1, :]
        out_ref[i] = part


def params():
    return pltpu.CompilerParams(
        vmem_limit_bytes=VMEM_LIMIT, dimension_semantics=("arbitrary",)
    )


def row_parts(row_count):
    parts, done = [], 0
    for share in np.cumsum(CHUNK_EIGHTHS):
        upto = row_count * int(share) // int(np.sum(CHUNK_EIGHTHS))
        if upto > done:
            parts.append((done, upto - done))
            done = upto
    return parts


def on_device(spectrum, radial_basis, cutoff, couplings, trap_potential, weights):
    local_modes, planes, degrees = spectrum.shape[1], spectrum.shape[3], spectrum.shape[4]
    radius_count = radial_basis.shape[1]
    axes = ("comp", "mr")
    components, mode_width = lax.axis_size("comp"), lax.axis_size("mr")
    device_count = components * mode_width
    mode_total = local_modes * mode_width
    lanes = 2 * planes
    block = math.gcd(local_modes, MODE_BLOCK)
    steps = local_modes // block

    mode_ids = lax.axis_index("mr") * local_modes + jnp.arange(local_modes, dtype=jnp.int32)
    signed = jnp.where(mode_ids < mode_total // 2, mode_ids, mode_ids - mode_total).astype(
        jnp.float32
    )
    degree_ids = jnp.arange(degrees, dtype=jnp.int32)
    energy = (
        2.0 * degree_ids.astype(jnp.float32)[None, :]
        + (jnp.abs(signed) + 1.0 - ROTATION * signed)[:, None]
    )
    kinetic_phase = TIMESTEP * energy
    kept_mask = (degree_ids[None, :] < cutoff[:, None]).astype(jnp.float32)
    kinetic_cos = jnp.cos(kinetic_phase) * kept_mask
    kinetic_sin = jnp.sin(kinetic_phase) * kept_mask
    table = spectral_tables(mode_total)
    to_turns = TIMESTEP / (2.0 * math.pi)
    lane_strength = jnp.repeat(couplings.T * to_turns, planes, axis=1)

    me = lax.axis_index(axes)
    parts = row_parts(radius_count // device_count)

    def basis_spec(rows, start):
        radii = rows * device_count
        assert start * device_count % radii == 0
        place = start * device_count // radii
        return pl.BlockSpec((block, radii, degrees), lambda i: (i, place, 0))

    def first_synthesis(start, rows):
        radii = rows * device_count
        return pl.pallas_call(
            functools.partial(first_synthesis_kernel, block, planes),
            grid=(steps,),
            out_shape=(
                jax.ShapeDtypeStruct((local_modes, lanes, degrees), jnp.bfloat16),
                jax.ShapeDtypeStruct((radii, local_modes, lanes), jnp.bfloat16),
            ),
            in_specs=[
                pl.BlockSpec((None, block, 2, planes, degrees), lambda i: (0, i, 0, 0, 0)),
                pl.BlockSpec((block, degrees), lambda i: (i, 0)),
                pl.BlockSpec((block, degrees), lambda i: (i, 0)),
                basis_spec(rows, start),
            ],
            out_specs=(
                pl.BlockSpec((block, lanes, degrees), lambda i: (i, 0, 0)),
                pl.BlockSpec((radii, block, lanes), lambda i: (0, i, 0)),
            ),
            scratch_shapes=[pltpu.VMEM((radii * block, lanes), jnp.float32)],
            compiler_params=params(),
            cost_estimate=pl.CostEstimate(
                flops=2 * local_modes * radii * degrees * lanes,
                bytes_accessed=6 * local_modes * lanes * degrees
                + 2 * local_modes * radii * (degrees + lanes),
                transcendentals=0,
            ),
            name="first_synthesis",
        )(spectrum, kinetic_cos, kinetic_sin, radial_basis)

    def synthesis(coeffs, start, rows):
        radii = rows * device_count
        return pl.pallas_call(
            functools.partial(synthesis_kernel, block),
            grid=(steps,),
            out_shape=jax.ShapeDtypeStruct((radii, local_modes, lanes), jnp.bfloat16),
            in_specs=[
                pl.BlockSpec((block, lanes, degrees), lambda i: (i, 0, 0)),
                basis_spec(rows, start),
            ],
            out_specs=pl.BlockSpec((radii, block, lanes), lambda i: (0, i, 0)),
            scratch_shapes=[pltpu.VMEM((radii * block, lanes), jnp.float32)],
            compiler_params=params(),
            cost_estimate=pl.CostEstimate(
                flops=2 * local_modes * radii * degrees * lanes,
                bytes_accessed=2 * local_modes * (lanes * degrees + radii * (degrees + lanes)),
                transcendentals=0,
            ),
            name="synthesis",
        )(coeffs, radial_basis)

    def physical(radial, start, rows):
        first_radius = start * device_count + me * rows
        trap = lax.dynamic_slice_in_dim(trap_potential, first_radius, rows) * to_turns
        weight = lax.dynamic_slice_in_dim(weights, first_radius, rows)
        shape = (components, mode_width, rows, local_modes, lanes)
        spec = pl.BlockSpec(
            (components, mode_width, 1, local_modes, lanes), lambda i: (0, 0, i, 0, 0)
        )
        tile = max(min(mode_total, 256), local_modes)
        return pl.pallas_call(
            functools.partial(physical_kernel, tile),
            grid=(rows,),
            out_shape=jax.ShapeDtypeStruct(shape, jnp.bfloat16),
            in_specs=[
                pl.BlockSpec(memory_space=pltpu.SMEM),
                pl.BlockSpec(memory_space=pltpu.SMEM),
                pl.BlockSpec((2, lanes), lambda i: (0, 0)),
                pl.BlockSpec((mode_total, 2 * mode_total), lambda i: (0, 0)),
                spec,
            ],
            out_specs=spec,
            scratch_shapes=[
                pltpu.VMEM((2 * mode_total, 2 * lanes), jnp.bfloat16),
                pltpu.VMEM((2 * mode_total, 2 * lanes), jnp.bfloat16),
            ],
            compiler_params=params(),
            cost_estimate=pl.CostEstimate(
                flops=16 * rows * mode_total * mode_total * lanes,
                bytes_accessed=8 * rows * mode_total * lanes + 4 * mode_total * mode_total,
                transcendentals=0,
            ),
            name="physical",
        )(trap, weight, lane_strength, table, radial.reshape(shape)).reshape(radial.shape)

    def analysis(fields, held, start, rows, last):
        radii = rows * device_count
        out_spec = pl.BlockSpec((block, lanes, degrees), lambda i: (i, 0, 0))
        operands = [fields, radial_basis, kept_mask]
        in_specs = [
            pl.BlockSpec((radii, block, lanes), lambda i: (0, i, 0)),
            basis_spec(rows, start),
            pl.BlockSpec((block, degrees), lambda i: (i, 0)),
        ]
        if held is not None:
            operands.append(held)
            in_specs.append(out_spec)
        return pl.pallas_call(
            functools.partial(analysis_kernel, block, held is None, last),
            grid=(steps,),
            out_shape=jax.ShapeDtypeStruct((local_modes, lanes, degrees), jnp.float32),
            in_specs=in_specs,
            out_specs=out_spec,
            scratch_shapes=[pltpu.VMEM((radii * block, lanes), jnp.float32)],
            input_output_aliases={} if held is None else {3: 0},
            compiler_params=params(),
            cost_estimate=pl.CostEstimate(
                flops=2 * local_modes * radii * degrees * lanes,
                bytes_accessed=2 * local_modes * radii * (degrees + lanes)
                + 8 * local_modes * lanes * degrees,
                transcendentals=0,
            ),
            name="analysis",
        )(*operands)

    def exchange(value):
        return lax.all_to_all(value, axes, split_axis=0, concat_axis=0, tiled=True)

    coeffs, synthesized = first_synthesis(*parts[0])
    arrived = []
    for k, part in enumerate(parts):
        if k > 0:
            synthesized = synthesis(coeffs, *part)
        arrived.append(exchange(synthesized))
    evolved = None
    returned = [exchange(physical(arrived[k], *part)) for k, part in enumerate(parts)]
    for k, part in enumerate(parts):
        evolved = analysis(returned[k], evolved, *part, k == len(parts) - 1)
    return evolved.reshape(1, local_modes, 2, planes, degrees)


def solution(mesh):
    in_specs = (P("comp", "mr", None, None, None), P("mr", None, None), P("mr"), P(), P(), P())
    out_specs = P("comp", "mr", None, None, None)
    return jax.shard_map(
        on_device, mesh=mesh, in_specs=in_specs, out_specs=out_specs, check_vma=False
    )
```

```python
import functools
import math

import jax
import jax.numpy as jnp
import numpy as np
from jax import lax
from jax.experimental import pallas as pl
from jax.experimental.pallas import tpu as pltpu
from jax.sharding import PartitionSpec as P

TIMESTEP = 0.5
ROTATION = 0.7
VMEM_LIMIT = 60 * 1024 * 1024
ROW_SHARES = (6, 26)
MODE_BLOCK = 16
MODE_PART = 16


def spectral_tables(mode_total):
    quarter = mode_total // 4
    ordinal = jnp.arange(quarter, dtype=jnp.int32)
    angle_ids = 4 * ordinal[None, :] + jnp.arange(4, dtype=jnp.int32)[:, None]
    product = angle_ids[:, :, None] * ordinal[None, None, :] % mode_total
    angles = product.astype(jnp.float32) * (2.0 * math.pi / mode_total)
    normalizer = 1.0 / math.sqrt(mode_total)
    cosine = (jnp.cos(angles) * normalizer).astype(jnp.bfloat16)
    sine = (jnp.sin(angles) * normalizer).astype(jnp.bfloat16)
    out = jnp.concatenate([cosine, sine], axis=2)
    back = jnp.concatenate([cosine.swapaxes(1, 2), sine.swapaxes(1, 2)], axis=2)
    return out, back


def kinetic_tables(mode_total, degrees):
    mode_ids = np.arange(mode_total)
    signed = np.where(mode_ids < mode_total // 2, mode_ids, mode_ids - mode_total)
    of_mode = TIMESTEP * (np.abs(signed) + 1.0 - ROTATION * signed)
    of_degree = TIMESTEP * 2.0 * np.arange(degrees)
    return tuple(
        jnp.asarray(np.stack([np.cos(angles), np.sin(angles)]), jnp.float32)
        for angles in (of_mode, of_degree)
    )


def half_turn_series():
    grid = np.cos(np.linspace(0.0, np.pi, 4001)) * 0.25
    grid = np.sort(np.concatenate([grid + 0.25, -(grid + 0.25)]))
    grid = grid[np.abs(grid) > 1e-9]
    square = grid * grid
    cheb = np.polynomial.chebyshev.Chebyshev
    sine = cheb.fit(square, np.sin(np.pi * grid) / grid, 4, domain=[0.0, 0.25])
    cosine = cheb.fit(square, np.cos(np.pi * grid), 5, domain=[0.0, 0.25])
    poly = np.polynomial.polynomial.Polynomial
    return (
        [float(v) for v in sine.convert(kind=poly).coef],
        [float(v) for v in cosine.convert(kind=poly).coef],
    )


SINE_SERIES, COSINE_SERIES = half_turn_series()


def horner(series, square):
    total = jnp.full_like(square, series[-1])
    for term in reversed(series[:-1]):
        total = total * square + term
    return total


def cos_sin_of_turns(turns):
    rest = turns - jnp.round(turns)
    square = rest * rest
    sine = rest * horner(SINE_SERIES, square)
    cosine = horner(COSINE_SERIES, square)
    twice = sine + sine
    return 1.0 - twice * sine, twice * cosine


def swap_halves(value):
    return pltpu.roll(value, value.shape[-1] // 2, value.ndim - 1)


def synthesis_kernel(
    planes, first_ref, cutoff_ref, mode_ref, degree_ref, spectrum_ref, basis_ref, out_ref, stage
):
    part, radii, degrees = basis_ref.shape
    block = out_ref.shape[1]
    inner = pl.program_id(1)
    local = pl.program_id(0) * block + inner * part
    degree_ids = lax.broadcasted_iota(jnp.int32, (1, degrees), 1)
    for i in range(part):
        mode = first_ref[0] + local + i
        mode_cos, mode_sin = mode_ref[0, mode], mode_ref[1, mode]
        degree_cos, degree_sin = degree_ref[0:1, :], degree_ref[1:2, :]
        kept = degree_ids < cutoff_ref[local + i]
        cosine = jnp.where(kept, degree_cos * mode_cos - degree_sin * mode_sin, 0.0)
        sine = jnp.where(kept, degree_sin * mode_cos + degree_cos * mode_sin, 0.0)
        real = spectrum_ref[i, 0]
        imag = spectrum_ref[i, 1]
        coeffs = jnp.concatenate(
            [real * cosine + imag * sine, imag * cosine - real * sine], axis=0
        ).astype(jnp.bfloat16)
        stage[pl.ds(inner * part + i, radii, stride=block), :] = lax.dot_general(
            basis_ref[i], coeffs, (((1,), (1,)), ((), ())), preferred_element_type=jnp.float32
        )

    @pl.when(inner == pl.num_programs(1) - 1)
    def _():
        out_ref[...] = stage[...].reshape(out_ref.shape).astype(jnp.bfloat16)


def complex_sum(left, right):
    return left[0] + right[0], left[1] + right[1]


def complex_difference(left, right):
    return left[0] - right[0], left[1] - right[1]


def quarter_turn(value):
    return -value[1], value[0]


def physical_kernel(trap_ref, weight_ref, lanes_ref, table_ref, back_ref, x_ref, *refs):
    *out_refs, work, kick = refs
    row = pl.program_id(0)
    width, local_modes, lanes = x_ref.shape[1], x_ref.shape[3], x_ref.shape[4]
    quarter = width * local_modes // 4
    blocks = width // 4
    first = lax.broadcasted_iota(jnp.int32, (quarter, lanes), 1) < lanes // 2

    parts = []
    for j in range(4):
        own = slice(j * blocks, (j + 1) * blocks)
        low = x_ref[0, own, 0].reshape(quarter, lanes).astype(jnp.float32)
        high = x_ref[1, own, 0].reshape(quarter, lanes).astype(jnp.float32)
        parts.append(
            (
                jnp.where(first, low, swap_halves(high)),
                jnp.where(first, swap_halves(low), high),
            )
        )
    even, odd = complex_sum(parts[0], parts[2]), complex_sum(parts[1], parts[3])
    skew = quarter_turn(complex_difference(parts[1], parts[3]))
    rest = complex_difference(parts[0], parts[2])
    folded = (
        complex_sum(even, odd),
        complex_sum(rest, skew),
        complex_difference(even, odd),
        complex_difference(rest, skew),
    )
    for q, (real, imag) in enumerate(folded):
        real = real.astype(jnp.bfloat16)
        work[q, :quarter, :lanes] = real
        work[q, :quarter, lanes:] = imag.astype(jnp.bfloat16)
        work[q, quarter:, :lanes] = (-imag).astype(jnp.bfloat16)
        work[q, quarter:, lanes:] = real

    strength = lanes_ref[0:1, :]
    cross = lanes_ref[1:2, :]
    trap = trap_ref[row]
    weight = weight_ref[row]
    for q in range(4):
        psi = jnp.dot(table_ref[q], work[q], preferred_element_type=jnp.float32)
        real, imag = psi[:, :lanes], psi[:, lanes:]
        density = real * real + imag * imag
        turns = strength * density + cross * swap_halves(density) + trap
        cosine, sine = cos_sin_of_turns(turns)
        kick_real = real * cosine + imag * sine
        kick_imag = (imag * cosine - real * sine).astype(jnp.bfloat16)
        kick[q, :quarter, :lanes] = kick_real.astype(jnp.bfloat16)
        kick[q, :quarter, lanes:] = kick_imag
        kick[q, quarter:, :lanes] = kick_imag
        kick[q, quarter:, lanes:] = (-kick_real).astype(jnp.bfloat16)

    backs = []
    for q in range(4):
        back = jnp.dot(back_ref[q], kick[q], preferred_element_type=jnp.float32)
        backs.append((back[:, :lanes], back[:, lanes:]))
    even, odd = complex_sum(backs[0], backs[2]), complex_sum(backs[1], backs[3])
    skew = quarter_turn(complex_difference(backs[1], backs[3]))
    rest = complex_difference(backs[0], backs[2])
    unfolded = (
        complex_sum(even, odd),
        complex_difference(rest, skew),
        complex_difference(even, odd),
        complex_sum(rest, skew),
    )
    for j, (real, imag) in enumerate(unfolded):
        own = slice(j * blocks, (j + 1) * blocks)
        real, imag = real * weight, imag * weight
        low = jnp.where(first, real, swap_halves(imag)).astype(jnp.bfloat16)
        high = jnp.where(first, swap_halves(real), imag).astype(jnp.bfloat16)
        low = low.reshape(blocks, local_modes, lanes)
        high = high.reshape(blocks, local_modes, lanes)
        skip = 0
        for out_ref in out_refs:
            count = out_ref.shape[3]
            out_ref[0, own, 0] = low[:, skip : skip + count]
            out_ref[1, own, 0] = high[:, skip : skip + count]
            skip += count


def analysis_kernel(skip, first, last, cutoff_ref, fields_ref, basis_ref, *refs):
    out_ref, stage = refs[-2:]
    block, radii, degrees = basis_ref.shape
    local = skip + pl.program_id(0) * block
    step = pl.program_id(1)
    stage[...] = fields_ref[...].astype(jnp.float32).reshape(stage.shape)

    def add_to(held_ref):
        for i in range(block):
            field = stage[pl.ds(i, radii, stride=block), :].astype(jnp.bfloat16)
            part = lax.dot_general(
                field, basis_ref[i], (((0,), (0,)), ((), ())), preferred_element_type=jnp.float32
            )
            out_ref[i] = part if held_ref is None else part + held_ref[i]

    @pl.when(step == 0)
    def _():
        add_to(None if first else refs[0])

    @pl.when(step > 0)
    def _():
        add_to(out_ref)

    if last:

        @pl.when(step == pl.num_programs(1) - 1)
        def _():
            degree_ids = lax.broadcasted_iota(jnp.int32, (1, degrees), 1)
            for i in range(block):
                kept = (degree_ids < cutoff_ref[local + i]).astype(jnp.float32)
                out_ref[i] = out_ref[i] * kept


def params(grid_rank=1):
    return pltpu.CompilerParams(
        vmem_limit_bytes=VMEM_LIMIT, dimension_semantics=("arbitrary",) * grid_rank
    )


def row_parts(row_count):
    parts, done = [], 0
    for share in np.cumsum(ROW_SHARES):
        upto = row_count * int(share) // int(np.sum(ROW_SHARES))
        if upto > done:
            parts.append((done, upto - done))
            done = upto
    return parts


def mode_parts(local_modes, block):
    if local_modes < 2 * block:
        return [(0, local_modes)]
    return [(0, local_modes - block), (local_modes - block, block)]


def on_device(spectrum, radial_basis, cutoff, couplings, trap_potential, weights):
    local_modes, planes, degrees = spectrum.shape[1], spectrum.shape[3], spectrum.shape[4]
    radius_count = radial_basis.shape[1]
    axes = ("comp", "mr")
    components, mode_width = lax.axis_size("comp"), lax.axis_size("mr")
    device_count = components * mode_width
    mode_total = local_modes * mode_width
    lanes = 2 * planes
    block = math.gcd(local_modes, MODE_BLOCK)

    first_mode = (lax.axis_index("mr") * local_modes).reshape(1).astype(jnp.int32)
    mode_phases, degree_phases = kinetic_tables(mode_total, degrees)
    table, back_table = spectral_tables(mode_total)
    to_turns = TIMESTEP / (2.0 * math.pi)
    lane_strength = jnp.repeat(couplings.T * to_turns, planes, axis=1)

    me = lax.axis_index(axes)
    parts = row_parts(radius_count // device_count)

    in_smem = pl.BlockSpec(memory_space=pltpu.SMEM)

    def synthesis(start, rows):
        radii = rows * device_count
        part = math.gcd(block, MODE_PART)
        per_block = block // part
        return pl.pallas_call(
            functools.partial(synthesis_kernel, planes),
            grid=(local_modes // block, per_block),
            out_shape=jax.ShapeDtypeStruct((radii, local_modes, lanes), jnp.bfloat16),
            in_specs=[
                in_smem,
                in_smem,
                in_smem,
                pl.BlockSpec((2, degrees), lambda i, j: (0, 0)),
                pl.BlockSpec(
                    (None, part, 2, planes, degrees), lambda i, j: (0, i * per_block + j, 0, 0, 0)
                ),
                pl.BlockSpec(
                    (pl.Element(part), pl.Element(radii), pl.Element(degrees)),
                    lambda i, j: ((i * per_block + j) * part, start * device_count, 0),
                ),
            ],
            out_specs=pl.BlockSpec((radii, block, lanes), lambda i, j: (0, i, 0)),
            scratch_shapes=[pltpu.VMEM((radii * block, lanes), jnp.float32)],
            compiler_params=params(2),
            cost_estimate=pl.CostEstimate(
                flops=2 * local_modes * radii * degrees * lanes,
                bytes_accessed=4 * local_modes * lanes * degrees
                + 2 * local_modes * radii * (degrees + lanes),
                transcendentals=0,
            ),
            name="synthesis",
        )(first_mode, cutoff, mode_phases, degree_phases, spectrum, radial_basis)

    def physical(radial, start, rows, groups):
        first_radius = start * device_count + me * rows
        trap = lax.dynamic_slice_in_dim(trap_potential, first_radius, rows) * to_turns
        weight = lax.dynamic_slice_in_dim(weights, first_radius, rows)
        quarter = mode_total // 4

        def shape(count):
            return (components, mode_width, rows, count, lanes)

        def spec(count):
            return pl.BlockSpec(
                (components, mode_width, 1, count, lanes), lambda i: (0, 0, i, 0, 0)
            )

        counts = [count for _, count in groups]
        kicked = pl.pallas_call(
            physical_kernel,
            grid=(rows,),
            out_shape=[jax.ShapeDtypeStruct(shape(count), jnp.bfloat16) for count in counts],
            in_specs=[
                in_smem,
                in_smem,
                pl.BlockSpec((2, lanes), lambda i: (0, 0)),
                pl.BlockSpec((4, quarter, 2 * quarter), lambda i: (0, 0, 0)),
                pl.BlockSpec((4, quarter, 2 * quarter), lambda i: (0, 0, 0)),
                spec(local_modes),
            ],
            out_specs=[spec(count) for count in counts],
            scratch_shapes=[
                pltpu.VMEM((4, 2 * quarter, 2 * lanes), jnp.bfloat16),
                pltpu.VMEM((4, 2 * quarter, 2 * lanes), jnp.bfloat16),
            ],
            compiler_params=params(),
            cost_estimate=pl.CostEstimate(
                flops=4 * rows * mode_total * mode_total * lanes,
                bytes_accessed=8 * rows * mode_total * lanes + 2 * mode_total * mode_total,
                transcendentals=0,
            ),
            name="physical",
        )(trap, weight, lane_strength, table, back_table, radial.reshape(shape(local_modes)))
        return [
            value.reshape(rows * device_count, count, lanes)
            for value, count in zip(kicked, counts)
        ]

    def analysis(fields, held, start, rows, last, skip):
        radii, count = fields.shape[:2]
        shift = skip // block
        steps = max(d for d in (1, 2, 4) if radii % (16 * d) == 0 and (d == 1 or radii // d >= 384))
        part = radii // steps
        out_spec = pl.BlockSpec((block, lanes, degrees), lambda i, j: (shift + i, 0, 0))
        operands = [cutoff, fields, radial_basis]
        in_specs = [
            in_smem,
            pl.BlockSpec((part, block, lanes), lambda i, j: (j, i, 0)),
            pl.BlockSpec(
                (pl.Element(block), pl.Element(part), pl.Element(degrees)),
                lambda i, j: (
                    skip + i * block,
                    pl.multiple_of(start * device_count + j * part, 16),
                    0,
                ),
            ),
        ]
        if held is not None:
            operands.append(held)
            in_specs.append(out_spec)
        return pl.pallas_call(
            functools.partial(analysis_kernel, skip, held is None, last),
            grid=(count // block, steps),
            out_shape=jax.ShapeDtypeStruct((local_modes, lanes, degrees), jnp.float32),
            in_specs=in_specs,
            out_specs=out_spec,
            scratch_shapes=[pltpu.VMEM((part * block, lanes), jnp.float32)],
            input_output_aliases={} if held is None else {3: 0},
            compiler_params=params(2),
            cost_estimate=pl.CostEstimate(
                flops=2 * count * radii * degrees * lanes,
                bytes_accessed=2 * count * radii * (degrees + lanes)
                + 8 * count * lanes * degrees,
                transcendentals=0,
            ),
            name="analysis",
        )(*operands)

    def exchange(value):
        return lax.all_to_all(value, axes, split_axis=0, concat_axis=0, tiled=True)

    arrived = [exchange(synthesis(*part)) for part in parts]
    returned = []
    for k, part in enumerate(parts):
        last = k == len(parts) - 1
        groups = mode_parts(local_modes, block) if last else [(0, local_modes)]
        for (skip, _), kicked in zip(groups, physical(arrived[k], *part, groups)):
            returned.append((exchange(kicked), part, last, skip))
    evolved = None
    for fields, part, last, skip in returned:
        evolved = analysis(fields, evolved, *part, last, skip)
    return evolved.reshape(1, local_modes, 2, planes, degrees)


def solution(mesh):
    in_specs = (P("comp", "mr", None, None, None), P("mr", None, None), P("mr"), P(), P(), P())
    out_specs = P("comp", "mr", None, None, None)
    return jax.shard_map(
        on_device, mesh=mesh, in_specs=in_specs, out_specs=out_specs, check_vma=False
    )
```

```python
import functools
import math

import jax
import jax.numpy as jnp
import numpy as np
from jax import lax
from jax.experimental import pallas as pl
from jax.experimental.pallas import tpu as pltpu
from jax.sharding import PartitionSpec as P

TIMESTEP = 0.5
ROTATION = 0.7
ROW_SHARES = (5, 27)
MODE_BLOCK = 16
LAST_MODES = 8


def spectral_tables(mode_total):
    quarter = mode_total // 4
    ordinal = jnp.arange(quarter, dtype=jnp.int32)
    angle_ids = 4 * ordinal[None, :] + jnp.arange(4, dtype=jnp.int32)[:, None]
    product = angle_ids[:, :, None] * ordinal[None, None, :] % mode_total
    angles = product.astype(jnp.float32) * (2.0 * math.pi / mode_total)
    normalizer = 1.0 / math.sqrt(mode_total)
    cosine = (jnp.cos(angles) * normalizer).astype(jnp.bfloat16)
    sine = (jnp.sin(angles) * normalizer).astype(jnp.bfloat16)
    out = jnp.concatenate([cosine, sine], axis=2)
    back = jnp.concatenate([cosine.swapaxes(1, 2), sine.swapaxes(1, 2)], axis=2)
    return out, back


def kinetic_tables(mode_total, degrees):
    mode_ids = np.arange(mode_total)
    signed = np.where(mode_ids < mode_total // 2, mode_ids, mode_ids - mode_total)
    of_mode = TIMESTEP * (np.abs(signed) + 1.0 - ROTATION * signed)
    of_degree = TIMESTEP * 2.0 * np.arange(degrees)
    return tuple(
        jnp.asarray(np.stack([np.cos(angles), np.sin(angles)]), jnp.float32)
        for angles in (of_mode, of_degree)
    )


def half_turn_series():
    grid = np.cos(np.linspace(0.0, np.pi, 4001)) * 0.25
    grid = np.sort(np.concatenate([grid + 0.25, -(grid + 0.25)]))
    grid = grid[np.abs(grid) > 1e-9]
    square = grid * grid
    cheb = np.polynomial.chebyshev.Chebyshev
    sine = cheb.fit(square, np.sin(np.pi * grid) / grid, 4, domain=[0.0, 0.25])
    cosine = cheb.fit(square, np.cos(np.pi * grid), 5, domain=[0.0, 0.25])
    poly = np.polynomial.polynomial.Polynomial
    return (
        [float(v) for v in sine.convert(kind=poly).coef],
        [float(v) for v in cosine.convert(kind=poly).coef],
    )


SINE_SERIES, COSINE_SERIES = half_turn_series()


def horner(series, square):
    total = jnp.full_like(square, series[-1])
    for term in reversed(series[:-1]):
        total = total * square + term
    return total


def cos_sin_of_turns(turns):
    rest = turns - jnp.round(turns)
    square = rest * rest
    sine = rest * horner(SINE_SERIES, square)
    cosine = horner(COSINE_SERIES, square)
    twice = sine + sine
    return 1.0 - twice * sine, twice * cosine


def swap_halves(value):
    return pltpu.roll(value, value.shape[-1] // 2, value.ndim - 1)


def synthesis_kernel(
    planes, first_ref, cutoff_ref, mode_ref, degree_ref, spectrum_ref, basis_ref, out_ref, stage
):
    block, radii, degrees = basis_ref.shape
    local = pl.program_id(0) * block
    degree_ids = lax.broadcasted_iota(jnp.int32, (1, degrees), 1)
    for i in range(block):
        mode = first_ref[0] + local + i
        mode_cos, mode_sin = mode_ref[0, mode], mode_ref[1, mode]
        degree_cos, degree_sin = degree_ref[0:1, :], degree_ref[1:2, :]
        kept = degree_ids < cutoff_ref[local + i]
        cosine = jnp.where(kept, degree_cos * mode_cos - degree_sin * mode_sin, 0.0)
        sine = jnp.where(kept, degree_sin * mode_cos + degree_cos * mode_sin, 0.0)
        real = spectrum_ref[i, 0]
        imag = spectrum_ref[i, 1]
        coeffs = jnp.concatenate(
            [real * cosine + imag * sine, imag * cosine - real * sine], axis=0
        ).astype(jnp.bfloat16)
        stage[pl.ds(i, radii, stride=block), :] = lax.dot_general(
            basis_ref[i], coeffs, (((1,), (1,)), ((), ())), preferred_element_type=jnp.float32
        )
    out_ref[...] = stage[...].reshape(out_ref.shape).astype(jnp.bfloat16)


def complex_sum(left, right):
    return left[0] + right[0], left[1] + right[1]


def complex_difference(left, right):
    return left[0] - right[0], left[1] - right[1]


def quarter_turn(value):
    return -value[1], value[0]


def physical_kernel(trap_ref, weight_ref, lanes_ref, table_ref, back_ref, x_ref, *refs):
    *out_refs, work, kick = refs
    row = pl.program_id(0)
    width, local_modes, lanes = x_ref.shape[1], x_ref.shape[3], x_ref.shape[4]
    quarter = width * local_modes // 4
    blocks = width // 4
    first = lax.broadcasted_iota(jnp.int32, (quarter, lanes), 1) < lanes // 2

    parts = []
    for j in range(4):
        own = slice(j * blocks, (j + 1) * blocks)
        low = x_ref[0, own, 0].reshape(quarter, lanes).astype(jnp.float32)
        high = x_ref[1, own, 0].reshape(quarter, lanes).astype(jnp.float32)
        parts.append(
            (
                jnp.where(first, low, swap_halves(high)),
                jnp.where(first, swap_halves(low), high),
            )
        )
    even, odd = complex_sum(parts[0], parts[2]), complex_sum(parts[1], parts[3])
    skew = quarter_turn(complex_difference(parts[1], parts[3]))
    rest = complex_difference(parts[0], parts[2])
    folded = (
        complex_sum(even, odd),
        complex_sum(rest, skew),
        complex_difference(even, odd),
        complex_difference(rest, skew),
    )
    for q, (real, imag) in enumerate(folded):
        real = real.astype(jnp.bfloat16)
        work[q, :quarter, :lanes] = real
        work[q, :quarter, lanes:] = imag.astype(jnp.bfloat16)
        work[q, quarter:, :lanes] = (-imag).astype(jnp.bfloat16)
        work[q, quarter:, lanes:] = real

    strength = lanes_ref[0:1, :]
    cross = lanes_ref[1:2, :]
    trap = trap_ref[row]
    weight = weight_ref[row]
    for q in range(4):
        psi = jnp.dot(table_ref[q], work[q], preferred_element_type=jnp.float32)
        real, imag = psi[:, :lanes], psi[:, lanes:]
        density = real * real + imag * imag
        turns = strength * density + cross * swap_halves(density) + trap
        cosine, sine = cos_sin_of_turns(turns)
        kick_real = real * cosine + imag * sine
        kick_imag = (imag * cosine - real * sine).astype(jnp.bfloat16)
        kick[q, :quarter, :lanes] = kick_real.astype(jnp.bfloat16)
        kick[q, :quarter, lanes:] = kick_imag
        kick[q, quarter:, :lanes] = kick_imag
        kick[q, quarter:, lanes:] = (-kick_real).astype(jnp.bfloat16)

    backs = []
    for q in range(4):
        back = jnp.dot(back_ref[q], kick[q], preferred_element_type=jnp.float32)
        backs.append((back[:, :lanes], back[:, lanes:]))
    even, odd = complex_sum(backs[0], backs[2]), complex_sum(backs[1], backs[3])
    skew = quarter_turn(complex_difference(backs[1], backs[3]))
    rest = complex_difference(backs[0], backs[2])
    unfolded = (
        complex_sum(even, odd),
        complex_difference(rest, skew),
        complex_difference(even, odd),
        complex_sum(rest, skew),
    )
    for j, (real, imag) in enumerate(unfolded):
        own = slice(j * blocks, (j + 1) * blocks)
        real, imag = real * weight, imag * weight
        low = jnp.where(first, real, swap_halves(imag)).reshape(blocks, local_modes, lanes)
        high = jnp.where(first, swap_halves(real), imag).reshape(blocks, local_modes, lanes)
        skip = 0
        for out_ref in out_refs:
            count = out_ref.shape[3]
            out_ref[0, own, 0] = low[:, skip : skip + count].astype(jnp.bfloat16)
            out_ref[1, own, 0] = high[:, skip : skip + count].astype(jnp.bfloat16)
            skip += count


def analysis_kernel(skip, first, last, cutoff_ref, fields_ref, basis_ref, *refs):
    out_ref, stage = refs[-2:]
    block, radii, degrees = basis_ref.shape
    local = skip + pl.program_id(0) * block
    step = pl.program_id(1)
    stage[...] = fields_ref[...].astype(jnp.float32).reshape(stage.shape)

    def add_to(held_ref):
        for i in range(block):
            field = stage[pl.ds(i, radii, stride=block), :].astype(jnp.bfloat16)
            part = lax.dot_general(
                field, basis_ref[i], (((0,), (0,)), ((), ())), preferred_element_type=jnp.float32
            )
            out_ref[i] = part if held_ref is None else part + held_ref[i]

    @pl.when(step == 0)
    def _():
        add_to(None if first else refs[0])

    @pl.when(step > 0)
    def _():
        add_to(out_ref)

    if last:

        @pl.when(step == pl.num_programs(1) - 1)
        def _():
            degree_ids = lax.broadcasted_iota(jnp.int32, (1, degrees), 1)
            for i in range(block):
                kept = (degree_ids < cutoff_ref[local + i]).astype(jnp.float32)
                out_ref[i] = out_ref[i] * kept


def hold_kernel(*refs):
    del refs


def hold(value, after):
    anywhere = pl.BlockSpec(memory_space=pl.ANY)
    return pl.pallas_call(
        hold_kernel,
        out_shape=jax.ShapeDtypeStruct(value.shape, value.dtype),
        in_specs=[anywhere] * (1 + len(after)),
        out_specs=anywhere,
        input_output_aliases={0: 0},
        name="hold",
    )(value, *after)


def params(grid_rank=1, mebibytes=60):
    return pltpu.CompilerParams(
        vmem_limit_bytes=mebibytes * 1024 * 1024, dimension_semantics=("arbitrary",) * grid_rank
    )


def row_parts(row_count):
    parts, done = [], 0
    for share in np.cumsum(ROW_SHARES):
        upto = row_count * int(share) // int(np.sum(ROW_SHARES))
        if upto > done:
            parts.append((done, upto - done))
            done = upto
    return parts


def mode_parts(local_modes, block):
    if local_modes < 2 * block:
        return [(0, local_modes)]
    return [(0, local_modes - LAST_MODES), (local_modes - LAST_MODES, LAST_MODES)]


def on_device(spectrum, radial_basis, cutoff, couplings, trap_potential, weights):
    local_modes, planes, degrees = spectrum.shape[1], spectrum.shape[3], spectrum.shape[4]
    radius_count = radial_basis.shape[1]
    axes = ("comp", "mr")
    components, mode_width = lax.axis_size("comp"), lax.axis_size("mr")
    device_count = components * mode_width
    mode_total = local_modes * mode_width
    lanes = 2 * planes
    block = math.gcd(local_modes, MODE_BLOCK)

    first_mode = (lax.axis_index("mr") * local_modes).reshape(1).astype(jnp.int32)
    mode_phases, degree_phases = kinetic_tables(mode_total, degrees)
    table, back_table = spectral_tables(mode_total)
    to_turns = TIMESTEP / (2.0 * math.pi)
    lane_strength = jnp.repeat(couplings.T * to_turns, planes, axis=1)

    me = lax.axis_index(axes)
    parts = row_parts(radius_count // device_count)

    in_smem = pl.BlockSpec(memory_space=pltpu.SMEM)

    def synthesis(start, rows):
        radii = rows * device_count
        return pl.pallas_call(
            functools.partial(synthesis_kernel, planes),
            grid=(local_modes // block,),
            out_shape=jax.ShapeDtypeStruct((radii, local_modes, lanes), jnp.bfloat16),
            in_specs=[
                in_smem,
                in_smem,
                in_smem,
                pl.BlockSpec((2, degrees), lambda i: (0, 0)),
                pl.BlockSpec((None, block, 2, planes, degrees), lambda i: (0, i, 0, 0, 0)),
                pl.BlockSpec(
                    (pl.Element(block), pl.Element(radii), pl.Element(degrees)),
                    lambda i: (i * block, start * device_count, 0),
                ),
            ],
            out_specs=pl.BlockSpec((radii, block, lanes), lambda i: (0, i, 0)),
            scratch_shapes=[pltpu.VMEM((radii * block, lanes), jnp.float32)],
            compiler_params=params(),
            cost_estimate=pl.CostEstimate(
                flops=2 * local_modes * radii * degrees * lanes,
                bytes_accessed=4 * local_modes * lanes * degrees
                + 2 * local_modes * radii * (degrees + lanes),
                transcendentals=0,
            ),
            name="synthesis",
        )(first_mode, cutoff, mode_phases, degree_phases, spectrum, radial_basis)

    def physical(radial, start, rows, groups):
        first_radius = start * device_count + me * rows
        trap = lax.dynamic_slice_in_dim(trap_potential, first_radius, rows) * to_turns
        weight = lax.dynamic_slice_in_dim(weights, first_radius, rows)
        quarter = mode_total // 4

        def shape(count):
            return (components, mode_width, rows, count, lanes)

        def spec(count):
            return pl.BlockSpec(
                (components, mode_width, 1, count, lanes), lambda i: (0, 0, i, 0, 0)
            )

        counts = [count for _, count in groups]
        kicked = pl.pallas_call(
            physical_kernel,
            grid=(rows,),
            out_shape=[jax.ShapeDtypeStruct(shape(count), jnp.bfloat16) for count in counts],
            in_specs=[
                in_smem,
                in_smem,
                pl.BlockSpec((2, lanes), lambda i: (0, 0)),
                pl.BlockSpec((4, quarter, 2 * quarter), lambda i: (0, 0, 0)),
                pl.BlockSpec((4, quarter, 2 * quarter), lambda i: (0, 0, 0)),
                spec(local_modes),
            ],
            out_specs=[spec(count) for count in counts],
            scratch_shapes=[
                pltpu.VMEM((4, 2 * quarter, 2 * lanes), jnp.bfloat16),
                pltpu.VMEM((4, 2 * quarter, 2 * lanes), jnp.bfloat16),
            ],
            compiler_params=params(1, 48),
            cost_estimate=pl.CostEstimate(
                flops=4 * rows * mode_total * mode_total * lanes,
                bytes_accessed=8 * rows * mode_total * lanes + 2 * mode_total * mode_total,
                transcendentals=0,
            ),
            name="physical",
        )(trap, weight, lane_strength, table, back_table, radial.reshape(shape(local_modes)))
        return [
            value.reshape(rows * device_count, count, lanes)
            for value, count in zip(kicked, counts)
        ]

    def analysis(fields, held, start, rows, last, skip):
        radii, count = fields.shape[:2]
        block = math.gcd(count, MODE_BLOCK)
        shift = skip // block
        steps = max(d for d in (1, 2, 4) if radii % (16 * d) == 0 and (d == 1 or radii // d >= 384))
        part = radii // steps
        out_spec = pl.BlockSpec((block, lanes, degrees), lambda i, j: (shift + i, 0, 0))
        operands = [cutoff, fields, radial_basis]
        in_specs = [
            in_smem,
            pl.BlockSpec((part, block, lanes), lambda i, j: (j, i, 0)),
            pl.BlockSpec(
                (pl.Element(block), pl.Element(part), pl.Element(degrees)),
                lambda i, j: (
                    skip + i * block,
                    pl.multiple_of(start * device_count + j * part, 16),
                    0,
                ),
            ),
        ]
        if held is not None:
            operands.append(held)
            in_specs.append(out_spec)
        return pl.pallas_call(
            functools.partial(analysis_kernel, skip, held is None, last),
            grid=(count // block, steps),
            out_shape=jax.ShapeDtypeStruct((local_modes, lanes, degrees), jnp.float32),
            in_specs=in_specs,
            out_specs=out_spec,
            scratch_shapes=[pltpu.VMEM((part * block, lanes), jnp.float32)],
            input_output_aliases={} if held is None else {3: 0},
            compiler_params=params(2, 50),
            cost_estimate=pl.CostEstimate(
                flops=2 * count * radii * degrees * lanes,
                bytes_accessed=2 * count * radii * (degrees + lanes)
                + 8 * count * lanes * degrees,
                transcendentals=0,
            ),
            name="analysis",
        )(*operands)

    def exchange(value):
        return lax.all_to_all(value, axes, split_axis=0, concat_axis=0, tiled=True)

    arrived = [exchange(synthesis(*part)) for part in parts]
    kicked = []
    for k, part in enumerate(parts):
        last = k == len(parts) - 1
        groups = mode_parts(local_modes, block) if last else [(0, local_modes)]
        for (skip, _), values in zip(groups, physical(arrived[k], *part, groups)):
            kicked.append((values, part, last, skip))
    evolved, before, waiting = None, None, None
    for values, part, last, skip in kicked:
        if before is not None:
            values = hold(values, [before])
        fields = exchange(values)
        if waiting is not None:
            before = evolved = analysis(waiting[0], evolved, *waiting[1:])
        waiting = (fields, *part, last, skip)
    evolved = analysis(waiting[0], evolved, *waiting[1:])
    return evolved.reshape(1, local_modes, 2, planes, degrees)


def solution(mesh):
    in_specs = (P("comp", "mr", None, None, None), P("mr", None, None), P("mr"), P(), P(), P())
    out_specs = P("comp", "mr", None, None, None)
    return jax.shard_map(
        on_device, mesh=mesh, in_specs=in_specs, out_specs=out_specs, check_vma=False
    )
```

```python
import functools
import math

import jax
import jax.numpy as jnp
import numpy as np
from jax import lax
from jax.experimental import pallas as pl
from jax.experimental.pallas import tpu as pltpu
from jax.sharding import Mesh
from jax.sharding import PartitionSpec as P

TIMESTEP = 0.5
ROTATION = 0.7
ROW_SHARES = (5, 27)
MODE_BLOCK = 16
LAST_MODES = 8


def spectral_tables(mode_total):
    quarter = mode_total // 4
    ordinal = jnp.arange(quarter, dtype=jnp.int32)
    angle_ids = 4 * ordinal[None, :] + jnp.arange(4, dtype=jnp.int32)[:, None]
    product = angle_ids[:, :, None] * ordinal[None, None, :] % mode_total
    angles = product.astype(jnp.float32) * (2.0 * math.pi / mode_total)
    normalizer = 1.0 / math.sqrt(mode_total)
    cosine = (jnp.cos(angles) * normalizer).astype(jnp.bfloat16)
    sine = (jnp.sin(angles) * normalizer).astype(jnp.bfloat16)
    out = jnp.concatenate([cosine, sine], axis=2)
    back = jnp.concatenate([cosine.swapaxes(1, 2), sine.swapaxes(1, 2)], axis=2)
    return out, back


def kinetic_tables(mode_total, degrees):
    mode_ids = np.arange(mode_total)
    signed = np.where(mode_ids < mode_total // 2, mode_ids, mode_ids - mode_total)
    of_mode = TIMESTEP * (np.abs(signed) + 1.0 - ROTATION * signed)
    of_degree = TIMESTEP * 2.0 * np.arange(degrees)
    return tuple(
        jnp.asarray(np.stack([np.cos(angles), np.sin(angles)]), jnp.float32)
        for angles in (of_mode, of_degree)
    )


def half_turn_series():
    grid = np.cos(np.linspace(0.0, np.pi, 4001)) * 0.25
    grid = np.sort(np.concatenate([grid + 0.25, -(grid + 0.25)]))
    grid = grid[np.abs(grid) > 1e-9]
    square = grid * grid
    cheb = np.polynomial.chebyshev.Chebyshev
    sine = cheb.fit(square, np.sin(np.pi * grid) / grid, 4, domain=[0.0, 0.25])
    cosine = cheb.fit(square, np.cos(np.pi * grid), 5, domain=[0.0, 0.25])
    poly = np.polynomial.polynomial.Polynomial
    return (
        [float(v) for v in sine.convert(kind=poly).coef],
        [float(v) for v in cosine.convert(kind=poly).coef],
    )


SINE_SERIES, COSINE_SERIES = half_turn_series()


def horner(series, square):
    total = jnp.full_like(square, series[-1])
    for term in reversed(series[:-1]):
        total = total * square + term
    return total


def cos_sin_of_turns(turns):
    rest = turns - jnp.round(turns)
    square = rest * rest
    sine = rest * horner(SINE_SERIES, square)
    cosine = horner(COSINE_SERIES, square)
    twice = sine + sine
    return 1.0 - twice * sine, twice * cosine


def swap_halves(value):
    return pltpu.roll(value, value.shape[-1] // 2, value.ndim - 1)


def relative_rows(place_ref, outer, group, size):
    for step in range(outer):
        for turn in range(group):
            device = (place_ref[0] ^ step) * group + (place_ref[1] ^ turn)
            yield step, turn, pl.multiple_of(device * size, size)


def synthesis_kernel(
    planes,
    outs,
    place_ref,
    first_ref,
    cutoff_ref,
    mode_ref,
    degree_ref,
    spectrum_ref,
    basis_ref,
    *refs,
):
    out_refs, stage = refs[-outs - 1 : -1], refs[-1]
    block, radii, degrees = basis_ref.shape
    local = pl.program_id(0) * block
    degree_ids = lax.broadcasted_iota(jnp.int32, (1, degrees), 1)
    for i in range(block):
        mode = first_ref[0] + local + i
        mode_cos, mode_sin = mode_ref[0, mode], mode_ref[1, mode]
        degree_cos, degree_sin = degree_ref[0:1, :], degree_ref[1:2, :]
        kept = degree_ids < cutoff_ref[local + i]
        cosine = jnp.where(kept, degree_cos * mode_cos - degree_sin * mode_sin, 0.0)
        sine = jnp.where(kept, degree_sin * mode_cos + degree_cos * mode_sin, 0.0)
        real = spectrum_ref[i, 0]
        imag = spectrum_ref[i, 1]
        coeffs = jnp.concatenate(
            [real * cosine + imag * sine, imag * cosine - real * sine], axis=0
        ).astype(jnp.bfloat16)
        stage[pl.ds(i, radii, stride=block), :] = lax.dot_general(
            basis_ref[i], coeffs, (((1,), (1,)), ((), ())), preferred_element_type=jnp.float32
        )
    if outs == 1:
        out_refs[0][...] = stage[...].reshape(out_refs[0].shape).astype(jnp.bfloat16)
        return
    group, rows, _, lanes = out_refs[0].shape
    size = rows * block
    for step, turn, start in relative_rows(place_ref, outs, group, size):
        piece = stage[pl.ds(start, size), :].astype(jnp.bfloat16)
        out_refs[step][turn] = piece.reshape(rows, block, lanes)


def complex_sum(left, right):
    return left[0] + right[0], left[1] + right[1]


def complex_difference(left, right):
    return left[0] - right[0], left[1] - right[1]


def quarter_turn(value):
    return -value[1], value[0]


def physical_kernel(
    relative,
    inner,
    outs,
    place_ref,
    trap_ref,
    weight_ref,
    lanes_ref,
    table_ref,
    back_ref,
    x_ref,
    *refs,
):
    out_refs, (work, kick) = refs[-outs - 2 : -2], refs[-2:]
    row = pl.program_id(0)
    local_modes, lanes = x_ref.shape[3:]
    quarter = inner * local_modes

    def block_at(component, j, i):
        if relative:
            return place_ref[1] ^ (component * inner + i), place_ref[0] ^ j
        return component, j * inner + i

    def field(component, j):
        pieces = [x_ref[(*block_at(component, j, i), 0)] for i in range(inner)]
        return jnp.concatenate(pieces, axis=0).astype(jnp.float32)

    first = lax.broadcasted_iota(jnp.int32, (quarter, lanes), 1) < lanes // 2

    parts = []
    for j in range(4):
        low, high = field(0, j), field(1, j)
        parts.append(
            (
                jnp.where(first, low, swap_halves(high)),
                jnp.where(first, swap_halves(low), high),
            )
        )
    even, odd = complex_sum(parts[0], parts[2]), complex_sum(parts[1], parts[3])
    skew = quarter_turn(complex_difference(parts[1], parts[3]))
    rest = complex_difference(parts[0], parts[2])
    folded = (
        complex_sum(even, odd),
        complex_sum(rest, skew),
        complex_difference(even, odd),
        complex_difference(rest, skew),
    )
    for q, (real, imag) in enumerate(folded):
        real = real.astype(jnp.bfloat16)
        work[q, :quarter, :lanes] = real
        work[q, :quarter, lanes:] = imag.astype(jnp.bfloat16)
        work[q, quarter:, :lanes] = (-imag).astype(jnp.bfloat16)
        work[q, quarter:, lanes:] = real

    strength = lanes_ref[0:1, :]
    cross = lanes_ref[1:2, :]
    trap = trap_ref[row]
    weight = weight_ref[row]
    for q in range(4):
        psi = jnp.dot(table_ref[q], work[q], preferred_element_type=jnp.float32)
        real, imag = psi[:, :lanes], psi[:, lanes:]
        density = real * real + imag * imag
        turns = strength * density + cross * swap_halves(density) + trap
        cosine, sine = cos_sin_of_turns(turns)
        kick_real = real * cosine + imag * sine
        kick_imag = (imag * cosine - real * sine).astype(jnp.bfloat16)
        kick[q, :quarter, :lanes] = kick_real.astype(jnp.bfloat16)
        kick[q, :quarter, lanes:] = kick_imag
        kick[q, quarter:, :lanes] = kick_imag
        kick[q, quarter:, lanes:] = (-kick_real).astype(jnp.bfloat16)

    backs = []
    for q in range(4):
        back = jnp.dot(back_ref[q], kick[q], preferred_element_type=jnp.float32)
        backs.append((back[:, :lanes], back[:, lanes:]))
    even, odd = complex_sum(backs[0], backs[2]), complex_sum(backs[1], backs[3])
    skew = quarter_turn(complex_difference(backs[1], backs[3]))
    rest = complex_difference(backs[0], backs[2])
    unfolded = (
        complex_sum(even, odd),
        complex_difference(rest, skew),
        complex_difference(even, odd),
        complex_sum(rest, skew),
    )
    for j, (real, imag) in enumerate(unfolded):
        real, imag = real * weight, imag * weight
        values = (
            jnp.where(first, real, swap_halves(imag)),
            jnp.where(first, swap_halves(real), imag),
        )
        for component, value in enumerate(values):
            for i in range(inner):
                skip = i * local_modes
                for out_ref in out_refs:
                    count = out_ref.shape[3]
                    out_ref[(*block_at(component, j, i), 0)] = value[skip : skip + count].astype(
                        jnp.bfloat16
                    )
                    skip += count


def analysis_kernel(skip, first, last, ins, place_ref, cutoff_ref, *refs):
    fields_refs, basis_ref, held_ref, (out_ref, stage) = (
        refs[:ins],
        refs[ins],
        refs[ins + 1],
        refs[-2:],
    )
    block, radii, degrees = basis_ref.shape
    local = skip + pl.program_id(0) * block
    step = pl.program_id(1)
    if ins == 1:
        stage[...] = fields_refs[0][...].astype(jnp.float32).reshape(stage.shape)
    else:
        group, rows = fields_refs[0].shape[:2]
        size = rows * block
        for distance, turn, start in relative_rows(place_ref, ins, group, size):
            piece = fields_refs[distance][turn].astype(jnp.float32)
            stage[pl.ds(start, size), :] = piece.reshape(size, stage.shape[1])

    def add_to(held_ref):
        for i in range(block):
            field = stage[pl.ds(i, radii, stride=block), :].astype(jnp.bfloat16)
            part = lax.dot_general(
                field, basis_ref[i], (((0,), (0,)), ((), ())), preferred_element_type=jnp.float32
            )
            out_ref[i] = part if held_ref is None else part + held_ref[i]

    @pl.when(step == 0)
    def _():
        add_to(None if first else held_ref)

    @pl.when(step > 0)
    def _():
        add_to(out_ref)

    if last:

        @pl.when(step == pl.num_programs(1) - 1)
        def _():
            degree_ids = lax.broadcasted_iota(jnp.int32, (1, degrees), 1)
            for i in range(block):
                kept = (degree_ids < cutoff_ref[local + i]).astype(jnp.float32)
                out_ref[i] = out_ref[i] * kept


def hold_kernel(*refs):
    del refs


def hold(value, after):
    anywhere = pl.BlockSpec(memory_space=pl.ANY)
    return pl.pallas_call(
        hold_kernel,
        out_shape=jax.ShapeDtypeStruct(value.shape, value.dtype),
        in_specs=[anywhere] * (1 + len(after)),
        out_specs=anywhere,
        input_output_aliases={0: 0},
        name="hold",
    )(value, *after)


def params(grid_rank=1, mebibytes=60):
    return pltpu.CompilerParams(
        vmem_limit_bytes=mebibytes * 1024 * 1024, dimension_semantics=("arbitrary",) * grid_rank
    )


def row_parts(row_count):
    parts, done = [], 0
    for share in np.cumsum(ROW_SHARES):
        upto = row_count * int(share) // int(np.sum(ROW_SHARES))
        if upto > done:
            parts.append((done, upto - done))
            done = upto
    return parts


def mode_parts(local_modes, block):
    if local_modes < 2 * block:
        return [(0, local_modes)]
    return [(0, local_modes - LAST_MODES), (local_modes - LAST_MODES, LAST_MODES)]


def on_device(spectrum, radial_basis, cutoff, couplings, trap_potential, weights):
    local_modes, planes, degrees = spectrum.shape[1], spectrum.shape[3], spectrum.shape[4]
    radius_count = radial_basis.shape[1]
    axes = ("comp", "hi", "lo")
    components, outer, inner = (lax.axis_size(name) for name in axes)
    mode_width, group = outer * inner, components * inner
    device_count = components * mode_width
    mode_total = local_modes * mode_width
    lanes = 2 * planes
    block = math.gcd(local_modes, MODE_BLOCK)

    first_mode = (lax.axis_index(("hi", "lo")) * local_modes).reshape(1).astype(jnp.int32)
    place = jnp.stack([lax.axis_index("hi"), lax.axis_index(("comp", "lo"))]).astype(jnp.int32)
    mode_phases, degree_phases = kinetic_tables(mode_total, degrees)
    table, back_table = spectral_tables(mode_total)
    to_turns = TIMESTEP / (2.0 * math.pi)
    lane_strength = jnp.repeat(couplings.T * to_turns, planes, axis=1)

    anywhere = pl.BlockSpec(memory_space=pl.ANY)
    parts = row_parts(radius_count // device_count)

    in_smem = pl.BlockSpec(memory_space=pltpu.SMEM)

    def synthesis(start, rows, relative, after):
        radii = rows * device_count
        if relative:
            shape, outs = (group, rows, local_modes, lanes), outer
            out_spec = pl.BlockSpec((group, rows, block, lanes), lambda i: (0, 0, i, 0))
        else:
            shape, outs = (radii, local_modes, lanes), 1
            out_spec = pl.BlockSpec((radii, block, lanes), lambda i: (0, i, 0))
        return pl.pallas_call(
            functools.partial(synthesis_kernel, planes, outs),
            grid=(local_modes // block,),
            out_shape=[jax.ShapeDtypeStruct(shape, jnp.bfloat16)] * outs,
            in_specs=[
                in_smem,
                in_smem,
                in_smem,
                in_smem,
                pl.BlockSpec((2, degrees), lambda i: (0, 0)),
                pl.BlockSpec((None, block, 2, planes, degrees), lambda i: (0, i, 0, 0, 0)),
                pl.BlockSpec(
                    (pl.Element(block), pl.Element(radii), pl.Element(degrees)),
                    lambda i: (i * block, start * device_count, 0),
                ),
                *[anywhere] * len(after),
            ],
            out_specs=[out_spec] * outs,
            scratch_shapes=[pltpu.VMEM((radii * block, lanes), jnp.float32)],
            compiler_params=params(),
            cost_estimate=pl.CostEstimate(
                flops=2 * local_modes * radii * degrees * lanes,
                bytes_accessed=4 * local_modes * lanes * degrees
                + 2 * local_modes * radii * (degrees + lanes),
                transcendentals=0,
            ),
            name="synthesis",
        )(
            place, first_mode, cutoff, mode_phases, degree_phases, spectrum, radial_basis, *after
        )

    def physical(radial, start, rows, groups, relative, after):
        me = lax.axis_index(("hi", "comp", "lo") if relative else axes)
        first_radius = start * device_count + me * rows
        trap = lax.dynamic_slice_in_dim(trap_potential, first_radius, rows) * to_turns
        weight = lax.dynamic_slice_in_dim(weights, first_radius, rows)
        quarter = mode_total // 4
        lead = (group, outer) if relative else (components, mode_width)

        def shape(count):
            return (*lead, rows, count, lanes)

        def spec(count):
            return pl.BlockSpec((*lead, 1, count, lanes), lambda i: (0, 0, i, 0, 0))

        counts = [count for _, count in groups]
        table_spec = pl.BlockSpec((4, quarter, 2 * quarter), lambda i: (0, 0, 0))
        return pl.pallas_call(
            functools.partial(physical_kernel, relative, inner, len(counts)),
            grid=(rows,),
            out_shape=[jax.ShapeDtypeStruct(shape(count), jnp.bfloat16) for count in counts],
            in_specs=[
                in_smem,
                in_smem,
                in_smem,
                pl.BlockSpec((2, lanes), lambda i: (0, 0)),
                table_spec,
                table_spec,
                spec(local_modes),
                *[anywhere] * len(after),
            ],
            out_specs=[spec(count) for count in counts],
            scratch_shapes=[
                pltpu.VMEM((4, 2 * quarter, 2 * lanes), jnp.bfloat16),
                pltpu.VMEM((4, 2 * quarter, 2 * lanes), jnp.bfloat16),
            ],
            compiler_params=params(),
            cost_estimate=pl.CostEstimate(
                flops=4 * rows * mode_total * mode_total * lanes,
                bytes_accessed=8 * rows * mode_total * lanes + 2 * mode_total * mode_total,
                transcendentals=0,
            ),
            name="physical",
        )(
            place,
            trap,
            weight,
            lane_strength,
            table,
            back_table,
            radial.reshape(shape(local_modes)),
            *after,
        )

    def analysis(fields, held, start, rows, last, skip):
        relative = len(fields) > 1
        radii, count = rows * device_count, fields[0].shape[-2]
        block = math.gcd(count, MODE_BLOCK)
        shift = skip // block
        halves = not relative and radii % 32 == 0 and radii >= 768
        steps = 2 if halves else 1
        part = radii // steps
        out_spec = pl.BlockSpec((block, lanes, degrees), lambda i, j: (shift + i, 0, 0))
        if relative:
            field_spec = pl.BlockSpec((group, rows, block, lanes), lambda i, j: (0, 0, i, 0))
        else:
            field_spec = pl.BlockSpec((part, block, lanes), lambda i, j: (j, i, 0))
        operands = [place, cutoff, *fields, radial_basis]
        in_specs = [
            in_smem,
            in_smem,
            *[field_spec] * len(fields),
            pl.BlockSpec(
                (pl.Element(block), pl.Element(part), pl.Element(degrees)),
                lambda i, j: (
                    skip + i * block,
                    pl.multiple_of(start * device_count + j * part, 16),
                    0,
                ),
            ),
        ]
        if held is not None:
            operands.append(held)
            in_specs.append(out_spec)
        return pl.pallas_call(
            functools.partial(analysis_kernel, skip, held is None, last, len(fields)),
            grid=(count // block, steps),
            out_shape=jax.ShapeDtypeStruct((local_modes, lanes, degrees), jnp.float32),
            in_specs=in_specs,
            out_specs=out_spec,
            scratch_shapes=[pltpu.VMEM((part * block, lanes), jnp.float32)],
            input_output_aliases={} if held is None else {len(operands) - 1: 0},
            compiler_params=params(2, 50),
            cost_estimate=pl.CostEstimate(
                flops=2 * count * radii * degrees * lanes,
                bytes_accessed=2 * count * radii * (degrees + lanes)
                + 8 * count * lanes * degrees,
                transcendentals=0,
            ),
            name="analysis",
        )(*operands)

    def exchange(value):
        return lax.all_to_all(value, axes, split_axis=0, concat_axis=0, tiled=True)

    def across(pieces):
        return [
            lax.ppermute(piece, "hi", [(i, i ^ step) for i in range(outer)]) if step else piece
            for step, piece in enumerate(pieces)
        ]

    def within(pieces):
        return [
            lax.ppermute(piece, ("comp", "lo"), [(i, i ^ turn) for i in range(group)])
            if turn
            else piece
            for turn, piece in enumerate(pieces)
        ]

    def swap_order(pieces):
        return [
            jnp.stack([piece[i] for piece in pieces]) for i in range(pieces[0].shape[0])
        ]

    small, large = parts
    all_modes = [(0, local_modes)]
    sent = synthesis(*small, True, [])
    synthesized = synthesis(*large, False, sent[:1])[0]
    arrived = across(sent)
    radial = exchange(hold(synthesized, arrived[1:]))
    near = jnp.stack(within(swap_order(arrived)))
    kicked = physical(near, *small, all_modes, True, [])[0]
    near = within([kicked[turn] for turn in range(group)])

    groups = mode_parts(local_modes, block)
    kicked = physical(radial, *large, groups, False, near[1:])
    sent = swap_order(near)
    sent = sent[:1] + [hold(piece, [radial]) for piece in sent[1:]]
    arrived = across(sent)

    evolved, waiting, after = None, (arrived, *small, False, 0), arrived[1:]
    for (skip, count), values in zip(groups, kicked):
        fields = exchange(hold(values.reshape(-1, count, lanes), after))
        evolved = analysis(waiting[0], evolved, *waiting[1:])
        waiting, after = ([fields], *large, True, skip), [evolved]
    evolved = analysis(waiting[0], evolved, *waiting[1:])
    return evolved.reshape(1, local_modes, 2, planes, degrees)


def solution(mesh):
    components, width = mesh.shape["comp"], mesh.shape["mr"]
    outer = math.gcd(width, 4)
    split_mesh = Mesh(
        mesh.devices.reshape(components, outer, width // outer), ("comp", "hi", "lo")
    )
    modes = ("hi", "lo")
    in_specs = (P("comp", modes, None, None, None), P(modes, None, None), P(modes), P(), P(), P())
    out_specs = P("comp", modes, None, None, None)
    return jax.shard_map(
        on_device, mesh=split_mesh, in_specs=in_specs, out_specs=out_specs, check_vma=False
    )
```

```python
import functools
import math

import jax
import jax.numpy as jnp
import numpy as np
from jax import lax
from jax.experimental import pallas as pl
from jax.experimental.pallas import tpu as pltpu
from jax.sharding import Mesh
from jax.sharding import PartitionSpec as P

TIMESTEP = 0.5
ROTATION = 0.7
ROW_SHARES = (5, 27)
MODE_BLOCK = 16
LAST_MODES = 8


def spectral_tables(mode_total):
    quarter = mode_total // 4
    ordinal = jnp.arange(quarter, dtype=jnp.int32)
    angle_ids = 4 * ordinal[None, :] + jnp.arange(4, dtype=jnp.int32)[:, None]
    product = angle_ids[:, :, None] * ordinal[None, None, :] % mode_total
    angles = product.astype(jnp.float32) * (2.0 * math.pi / mode_total)
    normalizer = 1.0 / math.sqrt(mode_total)
    cosine = (jnp.cos(angles) * normalizer).astype(jnp.bfloat16)
    sine = (jnp.sin(angles) * normalizer).astype(jnp.bfloat16)
    out = jnp.concatenate([cosine, sine], axis=2)
    back = jnp.concatenate([cosine.swapaxes(1, 2), sine.swapaxes(1, 2)], axis=2)
    return out, back


def kinetic_tables(mode_total, degrees):
    mode_ids = np.arange(mode_total)
    signed = np.where(mode_ids < mode_total // 2, mode_ids, mode_ids - mode_total)
    of_mode = TIMESTEP * (np.abs(signed) + 1.0 - ROTATION * signed)
    of_degree = TIMESTEP * 2.0 * np.arange(degrees)
    return tuple(
        jnp.asarray(np.stack([np.cos(angles), np.sin(angles)]), jnp.float32)
        for angles in (of_mode, of_degree)
    )


def half_turn_series():
    grid = np.cos(np.linspace(0.0, np.pi, 4001)) * 0.25
    grid = np.sort(np.concatenate([grid + 0.25, -(grid + 0.25)]))
    grid = grid[np.abs(grid) > 1e-9]
    square = grid * grid
    cheb = np.polynomial.chebyshev.Chebyshev
    sine = cheb.fit(square, np.sin(np.pi * grid) / grid, 4, domain=[0.0, 0.25])
    cosine = cheb.fit(square, np.cos(np.pi * grid), 5, domain=[0.0, 0.25])
    poly = np.polynomial.polynomial.Polynomial
    return (
        [float(v) for v in sine.convert(kind=poly).coef],
        [float(v) for v in cosine.convert(kind=poly).coef],
    )


SINE_SERIES, COSINE_SERIES = half_turn_series()


def horner(series, square):
    total = jnp.full_like(square, series[-1])
    for term in reversed(series[:-1]):
        total = total * square + term
    return total


def cos_sin_of_turns(turns):
    rest = turns - jnp.round(turns)
    square = rest * rest
    sine = rest * horner(SINE_SERIES, square)
    cosine = horner(COSINE_SERIES, square)
    twice = sine + sine
    return 1.0 - twice * sine, twice * cosine


def swap_halves(value):
    return pltpu.roll(value, value.shape[-1] // 2, value.ndim - 1)


def relative_rows(place_ref, outer, group, size, inner=None):
    for step in range(outer):
        for turn in range(group):
            outer_at, group_at = place_ref[0] ^ step, place_ref[1] ^ turn
            device = outer_at * group + group_at
            if inner is not None:
                device = lax.div(group_at, inner) * outer + outer_at
                device = device * inner + lax.rem(group_at, inner)
            yield step, turn, pl.multiple_of(device * size, size)


def synthesis_kernel(
    planes,
    outs,
    place_ref,
    first_ref,
    cutoff_ref,
    mode_ref,
    degree_ref,
    spectrum_ref,
    basis_ref,
    *refs,
):
    out_refs, stage = refs[-outs - 1 : -1], refs[-1]
    block, radii, degrees = basis_ref.shape
    local = pl.program_id(0) * block
    degree_ids = lax.broadcasted_iota(jnp.int32, (1, degrees), 1)
    for i in range(block):
        mode = first_ref[0] + local + i
        mode_cos, mode_sin = mode_ref[0, mode], mode_ref[1, mode]
        degree_cos, degree_sin = degree_ref[0:1, :], degree_ref[1:2, :]
        kept = degree_ids < cutoff_ref[local + i]
        cosine = jnp.where(kept, degree_cos * mode_cos - degree_sin * mode_sin, 0.0)
        sine = jnp.where(kept, degree_sin * mode_cos + degree_cos * mode_sin, 0.0)
        real = spectrum_ref[i, 0]
        imag = spectrum_ref[i, 1]
        coeffs = jnp.concatenate(
            [real * cosine + imag * sine, imag * cosine - real * sine], axis=0
        ).astype(jnp.bfloat16)
        stage[pl.ds(i, radii, stride=block), :] = lax.dot_general(
            basis_ref[i], coeffs, (((1,), (1,)), ((), ())), preferred_element_type=jnp.float32
        )
    if outs == 1:
        out_refs[0][...] = stage[...].reshape(out_refs[0].shape).astype(jnp.bfloat16)
        return
    group, rows, _, lanes = out_refs[0].shape
    size = rows * block
    for step, turn, start in relative_rows(place_ref, outs, group, size):
        piece = stage[pl.ds(start, size), :].astype(jnp.bfloat16)
        out_refs[step][turn] = piece.reshape(rows, block, lanes)


def complex_sum(left, right):
    return left[0] + right[0], left[1] + right[1]


def complex_difference(left, right):
    return left[0] - right[0], left[1] - right[1]


def quarter_turn(value):
    return -value[1], value[0]


def physical_kernel(
    relative,
    relative_outs,
    inner,
    place_ref,
    trap_ref,
    weight_ref,
    lanes_ref,
    table_ref,
    back_ref,
    x_ref,
    *refs,
):
    out_refs, (work, kick) = refs[-len(relative_outs) - 2 : -2], refs[-2:]
    row = pl.program_id(0)
    local_modes, lanes = x_ref.shape[3:]
    quarter = inner * local_modes

    def block_at(component, j, i, by_distance):
        if by_distance:
            return place_ref[1] ^ (component * inner + i), place_ref[0] ^ j
        return component, j * inner + i

    def field(component, j):
        pieces = [x_ref[(*block_at(component, j, i, relative), 0)] for i in range(inner)]
        return jnp.concatenate(pieces, axis=0).astype(jnp.float32)

    first = lax.broadcasted_iota(jnp.int32, (quarter, lanes), 1) < lanes // 2

    parts = []
    for j in range(4):
        low, high = field(0, j), field(1, j)
        parts.append(
            (
                jnp.where(first, low, swap_halves(high)),
                jnp.where(first, swap_halves(low), high),
            )
        )
    even, odd = complex_sum(parts[0], parts[2]), complex_sum(parts[1], parts[3])
    skew = quarter_turn(complex_difference(parts[1], parts[3]))
    rest = complex_difference(parts[0], parts[2])
    folded = (
        complex_sum(even, odd),
        complex_sum(rest, skew),
        complex_difference(even, odd),
        complex_difference(rest, skew),
    )
    for q, (real, imag) in enumerate(folded):
        real = real.astype(jnp.bfloat16)
        work[q, :quarter, :lanes] = real
        work[q, :quarter, lanes:] = imag.astype(jnp.bfloat16)
        work[q, quarter:, :lanes] = (-imag).astype(jnp.bfloat16)
        work[q, quarter:, lanes:] = real

    strength = lanes_ref[0:1, :]
    cross = lanes_ref[1:2, :]
    trap = trap_ref[row]
    weight = weight_ref[row]
    for q in range(4):
        psi = jnp.dot(table_ref[q], work[q], preferred_element_type=jnp.float32)
        real, imag = psi[:, :lanes], psi[:, lanes:]
        density = real * real + imag * imag
        turns = strength * density + cross * swap_halves(density) + trap
        cosine, sine = cos_sin_of_turns(turns)
        kick_real = real * cosine + imag * sine
        kick_imag = (imag * cosine - real * sine).astype(jnp.bfloat16)
        kick[q, :quarter, :lanes] = kick_real.astype(jnp.bfloat16)
        kick[q, :quarter, lanes:] = kick_imag
        kick[q, quarter:, :lanes] = kick_imag
        kick[q, quarter:, lanes:] = (-kick_real).astype(jnp.bfloat16)

    backs = []
    for q in range(4):
        back = jnp.dot(back_ref[q], kick[q], preferred_element_type=jnp.float32)
        backs.append((back[:, :lanes], back[:, lanes:]))
    even, odd = complex_sum(backs[0], backs[2]), complex_sum(backs[1], backs[3])
    skew = quarter_turn(complex_difference(backs[1], backs[3]))
    rest = complex_difference(backs[0], backs[2])
    unfolded = (
        complex_sum(even, odd),
        complex_difference(rest, skew),
        complex_difference(even, odd),
        complex_sum(rest, skew),
    )
    for j, (real, imag) in enumerate(unfolded):
        real, imag = real * weight, imag * weight
        values = (
            jnp.where(first, real, swap_halves(imag)),
            jnp.where(first, swap_halves(real), imag),
        )
        for component, value in enumerate(values):
            for i in range(inner):
                skip = i * local_modes
                for out_ref, by_distance in zip(out_refs, relative_outs):
                    count = out_ref.shape[3]
                    at = (*block_at(component, j, i, by_distance), 0)
                    out_ref[at] = value[skip : skip + count].astype(jnp.bfloat16)
                    skip += count


def analysis_kernel(skip, first, last, ins, inner, place_ref, cutoff_ref, *refs):
    fields_refs, basis_ref, held_ref, (out_ref, stage) = (
        refs[:ins],
        refs[ins],
        refs[ins + 1],
        refs[-2:],
    )
    block, radii, degrees = basis_ref.shape
    local = skip + pl.program_id(0) * block
    step = pl.program_id(1)
    if ins == 1:
        stage[...] = fields_refs[0][...].astype(jnp.float32).reshape(stage.shape)
    else:
        group, rows = fields_refs[0].shape[:2]
        size = rows * block
        for distance, turn, start in relative_rows(place_ref, ins, group, size, inner):
            piece = fields_refs[distance][turn].astype(jnp.float32)
            stage[pl.ds(start, size), :] = piece.reshape(size, stage.shape[1])

    def add_to(held_ref):
        for i in range(block):
            field = stage[pl.ds(i, radii, stride=block), :].astype(jnp.bfloat16)
            part = lax.dot_general(
                field, basis_ref[i], (((0,), (0,)), ((), ())), preferred_element_type=jnp.float32
            )
            out_ref[i] = part if held_ref is None else part + held_ref[i]

    @pl.when(step == 0)
    def _():
        add_to(None if first else held_ref)

    @pl.when(step > 0)
    def _():
        add_to(out_ref)

    if last:

        @pl.when(step == pl.num_programs(1) - 1)
        def _():
            degree_ids = lax.broadcasted_iota(jnp.int32, (1, degrees), 1)
            for i in range(block):
                kept = (degree_ids < cutoff_ref[local + i]).astype(jnp.float32)
                out_ref[i] = out_ref[i] * kept


def hold_kernel(*refs):
    del refs


def hold(value, after):
    anywhere = pl.BlockSpec(memory_space=pl.ANY)
    return pl.pallas_call(
        hold_kernel,
        out_shape=jax.ShapeDtypeStruct(value.shape, value.dtype),
        in_specs=[anywhere] * (1 + len(after)),
        out_specs=anywhere,
        input_output_aliases={0: 0},
        name="hold",
    )(value, *after)


def params(grid_rank=1, mebibytes=60):
    return pltpu.CompilerParams(
        vmem_limit_bytes=mebibytes * 1024 * 1024, dimension_semantics=("arbitrary",) * grid_rank
    )


def row_parts(row_count):
    parts, done = [], 0
    for share in np.cumsum(ROW_SHARES):
        upto = row_count * int(share) // int(np.sum(ROW_SHARES))
        if upto > done:
            parts.append((done, upto - done))
            done = upto
    return parts


def mode_parts(local_modes, block):
    if local_modes < 2 * block:
        return [(0, local_modes)]
    return [(0, local_modes - LAST_MODES), (local_modes - LAST_MODES, LAST_MODES)]


def on_device(spectrum, radial_basis, cutoff, couplings, trap_potential, weights):
    local_modes, planes, degrees = spectrum.shape[1], spectrum.shape[3], spectrum.shape[4]
    radius_count = radial_basis.shape[1]
    axes = ("comp", "hi", "lo")
    components, outer, inner = (lax.axis_size(name) for name in axes)
    mode_width, group = outer * inner, components * inner
    device_count = components * mode_width
    mode_total = local_modes * mode_width
    lanes = 2 * planes
    block = math.gcd(local_modes, MODE_BLOCK)

    first_mode = (lax.axis_index(("hi", "lo")) * local_modes).reshape(1).astype(jnp.int32)
    place = jnp.stack([lax.axis_index("hi"), lax.axis_index(("comp", "lo"))]).astype(jnp.int32)
    mode_phases, degree_phases = kinetic_tables(mode_total, degrees)
    table, back_table = spectral_tables(mode_total)
    to_turns = TIMESTEP / (2.0 * math.pi)
    lane_strength = jnp.repeat(couplings.T * to_turns, planes, axis=1)

    anywhere = pl.BlockSpec(memory_space=pl.ANY)
    parts = row_parts(radius_count // device_count)

    in_smem = pl.BlockSpec(memory_space=pltpu.SMEM)

    def synthesis(start, rows, relative, after):
        radii = rows * device_count
        if relative:
            shape, outs = (group, rows, local_modes, lanes), outer
            out_spec = pl.BlockSpec((group, rows, block, lanes), lambda i: (0, 0, i, 0))
        else:
            shape, outs = (radii, local_modes, lanes), 1
            out_spec = pl.BlockSpec((radii, block, lanes), lambda i: (0, i, 0))
        return pl.pallas_call(
            functools.partial(synthesis_kernel, planes, outs),
            grid=(local_modes // block,),
            out_shape=[jax.ShapeDtypeStruct(shape, jnp.bfloat16)] * outs,
            in_specs=[
                in_smem,
                in_smem,
                in_smem,
                in_smem,
                pl.BlockSpec((2, degrees), lambda i: (0, 0)),
                pl.BlockSpec((None, block, 2, planes, degrees), lambda i: (0, i, 0, 0, 0)),
                pl.BlockSpec(
                    (pl.Element(block), pl.Element(radii), pl.Element(degrees)),
                    lambda i: (i * block, start * device_count, 0),
                ),
                *[anywhere] * len(after),
            ],
            out_specs=[out_spec] * outs,
            scratch_shapes=[pltpu.VMEM((radii * block, lanes), jnp.float32)],
            compiler_params=params(),
            cost_estimate=pl.CostEstimate(
                flops=2 * local_modes * radii * degrees * lanes,
                bytes_accessed=4 * local_modes * lanes * degrees
                + 2 * local_modes * radii * (degrees + lanes),
                transcendentals=0,
            ),
            name="synthesis",
        )(
            place, first_mode, cutoff, mode_phases, degree_phases, spectrum, radial_basis, *after
        )

    def physical(radial, start, rows, groups, relative, relative_outs, after):
        me = lax.axis_index(("hi", "comp", "lo") if relative else axes)
        first_radius = start * device_count + me * rows
        trap = lax.dynamic_slice_in_dim(trap_potential, first_radius, rows) * to_turns
        weight = lax.dynamic_slice_in_dim(weights, first_radius, rows)
        quarter = mode_total // 4
        leads = {True: (group, outer), False: (components, mode_width)}

        def shape(count, by_distance):
            return (*leads[by_distance], rows, count, lanes)

        def spec(count, by_distance):
            return pl.BlockSpec(
                (*leads[by_distance], 1, count, lanes), lambda i: (0, 0, i, 0, 0)
            )

        outs = [(count, flag) for (_, count), flag in zip(groups, relative_outs)]
        table_spec = pl.BlockSpec((4, quarter, 2 * quarter), lambda i: (0, 0, 0))
        return pl.pallas_call(
            functools.partial(physical_kernel, relative, relative_outs, inner),
            grid=(rows,),
            out_shape=[jax.ShapeDtypeStruct(shape(*out), jnp.bfloat16) for out in outs],
            in_specs=[
                in_smem,
                in_smem,
                in_smem,
                pl.BlockSpec((2, lanes), lambda i: (0, 0)),
                table_spec,
                table_spec,
                spec(local_modes, relative),
                *[anywhere] * len(after),
            ],
            out_specs=[spec(*out) for out in outs],
            scratch_shapes=[
                pltpu.VMEM((4, 2 * quarter, 2 * lanes), jnp.bfloat16),
                pltpu.VMEM((4, 2 * quarter, 2 * lanes), jnp.bfloat16),
            ],
            compiler_params=params(),
            cost_estimate=pl.CostEstimate(
                flops=4 * rows * mode_total * mode_total * lanes,
                bytes_accessed=8 * rows * mode_total * lanes + 2 * mode_total * mode_total,
                transcendentals=0,
            ),
            name="physical",
        )(
            place,
            trap,
            weight,
            lane_strength,
            table,
            back_table,
            radial.reshape(shape(local_modes, relative)),
            *after,
        )

    def analysis(fields, held, start, rows, last, skip, inner_order=None, after=()):
        relative = len(fields) > 1
        radii, count = rows * device_count, fields[0].shape[-2]
        block = math.gcd(count, MODE_BLOCK)
        shift = skip // block
        halves = not relative and radii % 32 == 0 and radii >= 768
        steps = 2 if halves else 1
        part = radii // steps
        out_spec = pl.BlockSpec((block, lanes, degrees), lambda i, j: (shift + i, 0, 0))
        if relative:
            field_spec = pl.BlockSpec((group, rows, block, lanes), lambda i, j: (0, 0, i, 0))
        else:
            field_spec = pl.BlockSpec((part, block, lanes), lambda i, j: (j, i, 0))
        operands = [place, cutoff, *fields, radial_basis]
        in_specs = [
            in_smem,
            in_smem,
            *[field_spec] * len(fields),
            pl.BlockSpec(
                (pl.Element(block), pl.Element(part), pl.Element(degrees)),
                lambda i, j: (
                    skip + i * block,
                    pl.multiple_of(start * device_count + j * part, 16),
                    0,
                ),
            ),
        ]
        if held is not None:
            operands.append(held)
            in_specs.append(out_spec)
        aliases = {} if held is None else {len(operands) - 1: 0}
        operands += after
        in_specs += [anywhere] * len(after)
        return pl.pallas_call(
            functools.partial(
                analysis_kernel, skip, held is None, last, len(fields), inner_order
            ),
            grid=(count // block, steps),
            out_shape=jax.ShapeDtypeStruct((local_modes, lanes, degrees), jnp.float32),
            in_specs=in_specs,
            out_specs=out_spec,
            scratch_shapes=[pltpu.VMEM((part * block, lanes), jnp.float32)],
            input_output_aliases=aliases,
            compiler_params=params(2, 50),
            cost_estimate=pl.CostEstimate(
                flops=2 * count * radii * degrees * lanes,
                bytes_accessed=2 * count * radii * (degrees + lanes)
                + 8 * count * lanes * degrees,
                transcendentals=0,
            ),
            name="analysis",
        )(*operands)

    def exchange(value):
        return lax.all_to_all(value, axes, split_axis=0, concat_axis=0, tiled=True)

    def across(pieces):
        return [
            lax.ppermute(piece, "hi", [(i, i ^ step) for i in range(outer)]) if step else piece
            for step, piece in enumerate(pieces)
        ]

    def within(pieces):
        return [
            lax.ppermute(piece, ("comp", "lo"), [(i, i ^ turn) for i in range(group)])
            if turn
            else piece
            for turn, piece in enumerate(pieces)
        ]

    def swap_order(pieces):
        return [
            jnp.stack([piece[i] for piece in pieces]) for i in range(pieces[0].shape[0])
        ]

    small, large = parts
    all_modes = [(0, local_modes)]
    sent = synthesis(*small, True, [])
    synthesized = synthesis(*large, False, sent[:1])[0]
    arrived = across(sent)
    radial = exchange(hold(synthesized, arrived[1:]))
    near = jnp.stack(within(swap_order(arrived)))
    kicked = physical(near, *small, all_modes, True, [True], [])[0]
    near = within([kicked[turn] for turn in range(group)])

    groups = mode_parts(local_modes, block)
    kicked = physical(radial, *large, groups, False, [False, True][: len(groups)], near[1:])
    sent = swap_order(near)
    sent = sent[:1] + [hold(piece, [radial]) for piece in sent[1:]]
    arrived = across(sent)

    late = []
    if len(groups) > 1:
        late = within([kicked[1][turn] for turn in range(group)])
    fields = exchange(hold(kicked[0].reshape(-1, groups[0][1], lanes), arrived[1:]))
    evolved = analysis(arrived, None, *small, False, 0, None, late[1:])
    evolved = analysis([fields], evolved, *large, True, 0)
    if len(groups) > 1:
        sent = swap_order(late)
        arrived = across(sent[:1] + [hold(piece, [fields]) for piece in sent[1:]])
        evolved = analysis(arrived, evolved, *large, True, groups[1][0], inner)
    return evolved.reshape(1, local_modes, 2, planes, degrees)


def solution(mesh):
    components, width = mesh.shape["comp"], mesh.shape["mr"]
    outer = math.gcd(width, 4)
    split_mesh = Mesh(
        mesh.devices.reshape(components, outer, width // outer), ("comp", "hi", "lo")
    )
    modes = ("hi", "lo")
    in_specs = (P("comp", modes, None, None, None), P(modes, None, None), P(modes), P(), P(), P())
    out_specs = P("comp", modes, None, None, None)
    return jax.shard_map(
        on_device, mesh=split_mesh, in_specs=in_specs, out_specs=out_specs, check_vma=False
    )
```

```python
import functools
import math

import jax
import jax.numpy as jnp
import numpy as np
from jax import lax
from jax.experimental import pallas as pl
from jax.experimental.pallas import tpu as pltpu
from jax.sharding import Mesh
from jax.sharding import PartitionSpec as P

TIMESTEP = 0.5
ROTATION = 0.7
ROW_SHARES = (5, 27)
MODE_BLOCK = 16
LAST_MODES = 8


def spectral_tables(mode_total):
    quarter = mode_total // 4
    ordinal = jnp.arange(quarter, dtype=jnp.int32)
    angle_ids = 4 * ordinal[None, :] + jnp.arange(4, dtype=jnp.int32)[:, None]
    product = angle_ids[:, :, None] * ordinal[None, None, :] % mode_total
    angles = product.astype(jnp.float32) * (2.0 * math.pi / mode_total)
    normalizer = 1.0 / math.sqrt(mode_total)
    cosine = (jnp.cos(angles) * normalizer).astype(jnp.bfloat16)
    sine = (jnp.sin(angles) * normalizer).astype(jnp.bfloat16)
    out = jnp.concatenate([cosine, sine], axis=2)
    back = jnp.concatenate([cosine.swapaxes(1, 2), sine.swapaxes(1, 2)], axis=2)
    return out, back


def kinetic_tables(mode_total, degrees):
    mode_ids = np.arange(mode_total)
    signed = np.where(mode_ids < mode_total // 2, mode_ids, mode_ids - mode_total)
    of_mode = TIMESTEP * (np.abs(signed) + 1.0 - ROTATION * signed)
    of_degree = TIMESTEP * 2.0 * np.arange(degrees)
    return tuple(
        jnp.asarray(np.stack([np.cos(angles), np.sin(angles)]), jnp.float32)
        for angles in (of_mode, of_degree)
    )


def half_turn_series():
    grid = np.cos(np.linspace(0.0, np.pi, 4001)) * 0.25
    grid = np.sort(np.concatenate([grid + 0.25, -(grid + 0.25)]))
    grid = grid[np.abs(grid) > 1e-9]
    square = grid * grid
    cheb = np.polynomial.chebyshev.Chebyshev
    sine = cheb.fit(square, np.sin(np.pi * grid) / grid, 4, domain=[0.0, 0.25])
    cosine = cheb.fit(square, np.cos(np.pi * grid), 4, domain=[0.0, 0.25])
    poly = np.polynomial.polynomial.Polynomial
    return (
        [float(v) for v in sine.convert(kind=poly).coef],
        [float(v) for v in cosine.convert(kind=poly).coef],
    )


SINE_SERIES, COSINE_SERIES = half_turn_series()


def horner(series, square):
    total = jnp.full_like(square, series[-1])
    for term in reversed(series[:-1]):
        total = total * square + term
    return total


def cos_sin_of_turns(turns):
    rest = turns - jnp.round(turns)
    square = rest * rest
    sine = rest * horner(SINE_SERIES, square)
    cosine = horner(COSINE_SERIES, square)
    twice = sine + sine
    return 1.0 - twice * sine, twice * cosine


def swap_halves(value):
    return pltpu.roll(value, value.shape[-1] // 2, value.ndim - 1)


def relative_rows(place_ref, outer, group, size, inner=None):
    for step in range(outer):
        for turn in range(group):
            outer_at, group_at = place_ref[0] ^ step, place_ref[1] ^ turn
            device = outer_at * group + group_at
            if inner is not None:
                device = lax.div(group_at, inner) * outer + outer_at
                device = device * inner + lax.rem(group_at, inner)
            yield step, turn, pl.multiple_of(device * size, size)


def synthesis_kernel(
    planes,
    outs,
    place_ref,
    first_ref,
    cutoff_ref,
    mode_ref,
    degree_ref,
    spectrum_ref,
    basis_ref,
    *refs,
):
    out_refs, stage = refs[-outs - 1 : -1], refs[-1]
    block, radii, degrees = basis_ref.shape
    local = pl.program_id(0) * block
    degree_ids = lax.broadcasted_iota(jnp.int32, (1, degrees), 1)
    for i in range(block):
        mode = first_ref[0] + local + i
        mode_cos, mode_sin = mode_ref[0, mode], mode_ref[1, mode]
        degree_cos, degree_sin = degree_ref[0:1, :], degree_ref[1:2, :]
        kept = degree_ids < cutoff_ref[local + i]
        cosine = jnp.where(kept, degree_cos * mode_cos - degree_sin * mode_sin, 0.0)
        sine = jnp.where(kept, degree_sin * mode_cos + degree_cos * mode_sin, 0.0)
        real = spectrum_ref[i, 0]
        imag = spectrum_ref[i, 1]
        coeffs = jnp.concatenate(
            [real * cosine + imag * sine, imag * cosine - real * sine], axis=0
        ).astype(jnp.bfloat16)
        stage[pl.ds(i, radii, stride=block), :] = lax.dot_general(
            basis_ref[i], coeffs, (((1,), (1,)), ((), ())), preferred_element_type=jnp.float32
        )
    if outs == 1:
        out_refs[0][...] = stage[...].reshape(out_refs[0].shape).astype(jnp.bfloat16)
        return
    group, rows, _, lanes = out_refs[0].shape
    size = rows * block
    for step, turn, start in relative_rows(place_ref, outs, group, size):
        piece = stage[pl.ds(start, size), :].astype(jnp.bfloat16)
        out_refs[step][turn] = piece.reshape(rows, block, lanes)


def complex_sum(left, right):
    return left[0] + right[0], left[1] + right[1]


def complex_difference(left, right):
    return left[0] - right[0], left[1] - right[1]


def quarter_turn(value):
    return -value[1], value[0]


def physical_kernel(
    relative,
    relative_outs,
    inner,
    place_ref,
    trap_ref,
    weight_ref,
    lanes_ref,
    table_ref,
    back_ref,
    x_ref,
    *refs,
):
    out_refs, (work, kick) = refs[-len(relative_outs) - 2 : -2], refs[-2:]
    row = pl.program_id(0)
    local_modes, lanes = x_ref.shape[3:]
    quarter = inner * local_modes

    def block_at(component, j, i, by_distance):
        if by_distance:
            return place_ref[1] ^ (component * inner + i), place_ref[0] ^ j
        return component, j * inner + i

    def field(component, j):
        pieces = [x_ref[(*block_at(component, j, i, relative), 0)] for i in range(inner)]
        return jnp.concatenate(pieces, axis=0).astype(jnp.float32)

    first = lax.broadcasted_iota(jnp.int32, (quarter, lanes), 1) < lanes // 2

    parts = []
    for j in range(4):
        low, high = field(0, j), field(1, j)
        parts.append(
            (
                jnp.where(first, low, swap_halves(high)),
                jnp.where(first, swap_halves(low), high),
            )
        )
    even, odd = complex_sum(parts[0], parts[2]), complex_sum(parts[1], parts[3])
    skew = quarter_turn(complex_difference(parts[1], parts[3]))
    rest = complex_difference(parts[0], parts[2])
    folded = (
        complex_sum(even, odd),
        complex_sum(rest, skew),
        complex_difference(even, odd),
        complex_difference(rest, skew),
    )
    for q, (real, imag) in enumerate(folded):
        real = real.astype(jnp.bfloat16)
        work[q, :quarter, :lanes] = real
        work[q, :quarter, lanes:] = imag.astype(jnp.bfloat16)
        work[q, quarter:, :lanes] = (-imag).astype(jnp.bfloat16)
        work[q, quarter:, lanes:] = real

    strength = lanes_ref[0:1, :]
    cross = lanes_ref[1:2, :]
    trap = trap_ref[row]
    weight = weight_ref[row]
    for q in range(4):
        psi = jnp.dot(table_ref[q], work[q], preferred_element_type=jnp.float32)
        real, imag = psi[:, :lanes], psi[:, lanes:]
        density = real * real + imag * imag
        turns = strength * density + cross * swap_halves(density) + trap
        cosine, sine = cos_sin_of_turns(turns)
        kick_real = real * cosine + imag * sine
        kick_imag = (imag * cosine - real * sine).astype(jnp.bfloat16)
        kick[q, :quarter, :lanes] = kick_real.astype(jnp.bfloat16)
        kick[q, :quarter, lanes:] = kick_imag
        kick[q, quarter:, :lanes] = kick_imag
        kick[q, quarter:, lanes:] = (-kick_real).astype(jnp.bfloat16)

    backs = []
    for q in range(4):
        back = jnp.dot(back_ref[q], kick[q], preferred_element_type=jnp.float32)
        backs.append((back[:, :lanes], back[:, lanes:]))
    even, odd = complex_sum(backs[0], backs[2]), complex_sum(backs[1], backs[3])
    skew = quarter_turn(complex_difference(backs[1], backs[3]))
    rest = complex_difference(backs[0], backs[2])
    unfolded = (
        complex_sum(even, odd),
        complex_difference(rest, skew),
        complex_difference(even, odd),
        complex_sum(rest, skew),
    )
    for j, (real, imag) in enumerate(unfolded):
        real, imag = real * weight, imag * weight
        values = (
            jnp.where(first, real, swap_halves(imag)),
            jnp.where(first, swap_halves(real), imag),
        )
        for component, value in enumerate(values):
            for i in range(inner):
                skip = i * local_modes
                for out_ref, by_distance in zip(out_refs, relative_outs):
                    count = out_ref.shape[3]
                    at = (*block_at(component, j, i, by_distance), 0)
                    out_ref[at] = value[skip : skip + count].astype(jnp.bfloat16)
                    skip += count


def analysis_kernel(skip, first, last, ins, inner, place_ref, cutoff_ref, *refs):
    fields_refs, basis_ref, held_ref, (out_ref, stage) = (
        refs[:ins],
        refs[ins],
        refs[ins + 1],
        refs[-2:],
    )
    block, radii, degrees = basis_ref.shape
    local = skip + pl.program_id(0) * block
    step = pl.program_id(1)
    if ins == 1:
        stage[...] = fields_refs[0][...].astype(jnp.float32).reshape(stage.shape)
    else:
        group, rows = fields_refs[0].shape[:2]
        size = rows * block
        for distance, turn, start in relative_rows(place_ref, ins, group, size, inner):
            piece = fields_refs[distance][turn].astype(jnp.float32)
            stage[pl.ds(start, size), :] = piece.reshape(size, stage.shape[1])

    def add_to(held_ref):
        for i in range(block):
            field = stage[pl.ds(i, radii, stride=block), :].astype(jnp.bfloat16)
            part = lax.dot_general(
                field, basis_ref[i], (((0,), (0,)), ((), ())), preferred_element_type=jnp.float32
            )
            out_ref[i] = part if held_ref is None else part + held_ref[i]

    @pl.when(step == 0)
    def _():
        add_to(None if first else held_ref)

    @pl.when(step > 0)
    def _():
        add_to(out_ref)

    if last:

        @pl.when(step == pl.num_programs(1) - 1)
        def _():
            degree_ids = lax.broadcasted_iota(jnp.int32, (1, degrees), 1)
            for i in range(block):
                kept = (degree_ids < cutoff_ref[local + i]).astype(jnp.float32)
                out_ref[i] = out_ref[i] * kept


def hold_kernel(*refs):
    del refs


def hold(value, after):
    anywhere = pl.BlockSpec(memory_space=pl.ANY)
    return pl.pallas_call(
        hold_kernel,
        out_shape=jax.ShapeDtypeStruct(value.shape, value.dtype),
        in_specs=[anywhere] * (1 + len(after)),
        out_specs=anywhere,
        input_output_aliases={0: 0},
        name="hold",
    )(value, *after)


def params(grid_rank=1, mebibytes=60):
    return pltpu.CompilerParams(
        vmem_limit_bytes=mebibytes * 1024 * 1024, dimension_semantics=("arbitrary",) * grid_rank
    )


def row_parts(row_count):
    parts, done = [], 0
    for share in np.cumsum(ROW_SHARES):
        upto = row_count * int(share) // int(np.sum(ROW_SHARES))
        if upto > done:
            parts.append((done, upto - done))
            done = upto
    return parts


def mode_parts(local_modes, block):
    if local_modes < 2 * block:
        return [(0, local_modes)]
    return [(0, local_modes - LAST_MODES), (local_modes - LAST_MODES, LAST_MODES)]


def on_device(spectrum, radial_basis, cutoff, couplings, trap_potential, weights):
    local_modes, planes, degrees = spectrum.shape[1], spectrum.shape[3], spectrum.shape[4]
    radius_count = radial_basis.shape[1]
    axes = ("comp", "hi", "lo")
    components, outer, inner = (lax.axis_size(name) for name in axes)
    mode_width, group = outer * inner, components * inner
    device_count = components * mode_width
    mode_total = local_modes * mode_width
    lanes = 2 * planes
    block = math.gcd(local_modes, MODE_BLOCK)

    first_mode = (lax.axis_index(("hi", "lo")) * local_modes).reshape(1).astype(jnp.int32)
    place = jnp.stack([lax.axis_index("hi"), lax.axis_index(("comp", "lo"))]).astype(jnp.int32)
    mode_phases, degree_phases = kinetic_tables(mode_total, degrees)
    table, back_table = spectral_tables(mode_total)
    to_turns = TIMESTEP / (2.0 * math.pi)
    lane_strength = jnp.repeat(couplings.T * to_turns, planes, axis=1)

    anywhere = pl.BlockSpec(memory_space=pl.ANY)
    parts = row_parts(radius_count // device_count)

    in_smem = pl.BlockSpec(memory_space=pltpu.SMEM)

    def synthesis(start, rows, relative, after):
        radii = rows * device_count
        if relative:
            shape, outs = (group, rows, local_modes, lanes), outer
            out_spec = pl.BlockSpec((group, rows, block, lanes), lambda i: (0, 0, i, 0))
        else:
            shape, outs = (radii, local_modes, lanes), 1
            out_spec = pl.BlockSpec((radii, block, lanes), lambda i: (0, i, 0))
        return pl.pallas_call(
            functools.partial(synthesis_kernel, planes, outs),
            grid=(local_modes // block,),
            out_shape=[jax.ShapeDtypeStruct(shape, jnp.bfloat16)] * outs,
            in_specs=[
                in_smem,
                in_smem,
                in_smem,
                in_smem,
                pl.BlockSpec((2, degrees), lambda i: (0, 0)),
                pl.BlockSpec((None, block, 2, planes, degrees), lambda i: (0, i, 0, 0, 0)),
                pl.BlockSpec(
                    (pl.Element(block), pl.Element(radii), pl.Element(degrees)),
                    lambda i: (i * block, start * device_count, 0),
                ),
                *[anywhere] * len(after),
            ],
            out_specs=[out_spec] * outs,
            scratch_shapes=[pltpu.VMEM((radii * block, lanes), jnp.float32)],
            compiler_params=params(),
            cost_estimate=pl.CostEstimate(
                flops=2 * local_modes * radii * degrees * lanes,
                bytes_accessed=4 * local_modes * lanes * degrees
                + 2 * local_modes * radii * (degrees + lanes),
                transcendentals=0,
            ),
            name="synthesis",
        )(
            place, first_mode, cutoff, mode_phases, degree_phases, spectrum, radial_basis, *after
        )

    def physical(radial, start, rows, groups, relative, relative_outs, after):
        me = lax.axis_index(("hi", "comp", "lo") if relative else axes)
        first_radius = start * device_count + me * rows
        trap = lax.dynamic_slice_in_dim(trap_potential, first_radius, rows) * to_turns
        weight = lax.dynamic_slice_in_dim(weights, first_radius, rows)
        quarter = mode_total // 4
        leads = {True: (group, outer), False: (components, mode_width)}

        def shape(count, by_distance):
            return (*leads[by_distance], rows, count, lanes)

        def spec(count, by_distance):
            return pl.BlockSpec(
                (*leads[by_distance], 1, count, lanes), lambda i: (0, 0, i, 0, 0)
            )

        outs = [(count, flag) for (_, count), flag in zip(groups, relative_outs)]
        table_spec = pl.BlockSpec((4, quarter, 2 * quarter), lambda i: (0, 0, 0))
        return pl.pallas_call(
            functools.partial(physical_kernel, relative, relative_outs, inner),
            grid=(rows,),
            out_shape=[jax.ShapeDtypeStruct(shape(*out), jnp.bfloat16) for out in outs],
            in_specs=[
                in_smem,
                in_smem,
                in_smem,
                pl.BlockSpec((2, lanes), lambda i: (0, 0)),
                table_spec,
                table_spec,
                spec(local_modes, relative),
                *[anywhere] * len(after),
            ],
            out_specs=[spec(*out) for out in outs],
            scratch_shapes=[
                pltpu.VMEM((4, 2 * quarter, 2 * lanes), jnp.bfloat16),
                pltpu.VMEM((4, 2 * quarter, 2 * lanes), jnp.bfloat16),
            ],
            compiler_params=params(),
            cost_estimate=pl.CostEstimate(
                flops=4 * rows * mode_total * mode_total * lanes,
                bytes_accessed=8 * rows * mode_total * lanes + 2 * mode_total * mode_total,
                transcendentals=0,
            ),
            name="physical",
        )(
            place,
            trap,
            weight,
            lane_strength,
            table,
            back_table,
            radial.reshape(shape(local_modes, relative)),
            *after,
        )

    def analysis(fields, held, start, rows, last, skip, inner_order=None, after=()):
        relative = len(fields) > 1
        radii, count = rows * device_count, fields[0].shape[-2]
        block = math.gcd(count, MODE_BLOCK)
        shift = skip // block
        halves = not relative and radii % 32 == 0 and radii * block >= 768 * MODE_BLOCK
        steps = 2 if halves else 1
        part = radii // steps
        out_spec = pl.BlockSpec((block, lanes, degrees), lambda i, j: (shift + i, 0, 0))
        if relative:
            field_spec = pl.BlockSpec((group, rows, block, lanes), lambda i, j: (0, 0, i, 0))
        else:
            field_spec = pl.BlockSpec((part, block, lanes), lambda i, j: (j, i, 0))
        operands = [place, cutoff, *fields, radial_basis]
        in_specs = [
            in_smem,
            in_smem,
            *[field_spec] * len(fields),
            pl.BlockSpec(
                (pl.Element(block), pl.Element(part), pl.Element(degrees)),
                lambda i, j: (
                    skip + i * block,
                    pl.multiple_of(start * device_count + j * part, 16),
                    0,
                ),
            ),
        ]
        if held is not None:
            operands.append(held)
            in_specs.append(out_spec)
        aliases = {} if held is None else {len(operands) - 1: 0}
        operands += after
        in_specs += [anywhere] * len(after)
        return pl.pallas_call(
            functools.partial(
                analysis_kernel, skip, held is None, last, len(fields), inner_order
            ),
            grid=(count // block, steps),
            out_shape=jax.ShapeDtypeStruct((local_modes, lanes, degrees), jnp.float32),
            in_specs=in_specs,
            out_specs=out_spec,
            scratch_shapes=[pltpu.VMEM((part * block, lanes), jnp.float32)],
            input_output_aliases=aliases,
            compiler_params=params(2, 50),
            cost_estimate=pl.CostEstimate(
                flops=2 * count * radii * degrees * lanes,
                bytes_accessed=2 * count * radii * (degrees + lanes)
                + 8 * count * lanes * degrees,
                transcendentals=0,
            ),
            name="analysis",
        )(*operands)

    def exchange(value):
        return lax.all_to_all(value, axes, split_axis=0, concat_axis=0, tiled=True)

    def across(pieces):
        return [
            lax.ppermute(piece, "hi", [(i, i ^ step) for i in range(outer)]) if step else piece
            for step, piece in enumerate(pieces)
        ]

    def within(pieces):
        return [
            lax.ppermute(piece, ("comp", "lo"), [(i, i ^ turn) for i in range(group)])
            if turn
            else piece
            for turn, piece in enumerate(pieces)
        ]

    def swap_order(pieces):
        return [
            jnp.stack([piece[i] for piece in pieces]) for i in range(pieces[0].shape[0])
        ]

    small, large = parts
    all_modes = [(0, local_modes)]
    sent = synthesis(*small, True, [])
    synthesized = synthesis(*large, False, sent[:1])[0]
    arrived = across(sent)
    radial = exchange(hold(synthesized, arrived[1:]))
    near = jnp.stack(within(swap_order(arrived)))
    kicked = physical(near, *small, all_modes, True, [True], [])[0]
    near = within([kicked[turn] for turn in range(group)])

    groups = mode_parts(local_modes, block)
    kicked = physical(radial, *large, groups, False, [False, True][: len(groups)], near[1:])
    sent = swap_order(near)
    sent = sent[:1] + [hold(piece, [radial]) for piece in sent[1:]]
    arrived = across(sent)

    late = []
    if len(groups) > 1:
        late = within([kicked[1][turn] for turn in range(group)])
    fields = exchange(hold(kicked[0].reshape(-1, groups[0][1], lanes), arrived[1:]))
    evolved = analysis(arrived, None, *small, False, 0, None, late[1:])
    evolved = analysis([fields], evolved, *large, True, 0)
    if len(groups) > 1:
        sent = swap_order(late)
        arrived = across(sent[:1] + [hold(piece, [fields]) for piece in sent[1:]])
        evolved = analysis(arrived, evolved, *large, True, groups[1][0], inner)
    return evolved.reshape(1, local_modes, 2, planes, degrees)


def solution(mesh):
    components, width = mesh.shape["comp"], mesh.shape["mr"]
    outer = math.gcd(width, 4)
    split_mesh = Mesh(
        mesh.devices.reshape(components, outer, width // outer), ("comp", "hi", "lo")
    )
    modes = ("hi", "lo")
    in_specs = (P("comp", modes, None, None, None), P(modes, None, None), P(modes), P(), P(), P())
    out_specs = P("comp", modes, None, None, None)
    return jax.shard_map(
        on_device, mesh=split_mesh, in_specs=in_specs, out_specs=out_specs, check_vma=False
    )
```
